32 devices in a mesh: seq: 4 (over y, x), row: 2 (over core), col: 4 (over z).
Axes of the slice: x: 2, y: 2, z: 4, core: 2. Of those that a mesh axis runs over, the one named last changes fastest.
Arguments:
- activations: bfloat16 [2048, 16384], P('seq', ('row', 'col')), may hold values from -1500 to 1500
- norm_gain: float32 [16384], P(('row', 'col')), may hold values from 0.1 to 1.9
- query_weight: bfloat16 [16384, 8192], P('row', 'col'), may hold values from -0.046875 to 0.046875
- kv_weight: bfloat16 [16384, 2, 512], P('row'), may hold values from -0.046875 to 0.046875
- out_weight: bfloat16 [8192, 16384], P('col', 'row'), may hold values from -0.5 to 0.5
- block_ids: int32 [2048], replicated, may hold values from 0 to 255, never falling along the last dimension, each value on 1 to 16 neighbouring positions
- clean_mask: int32 [2048], replicated, may hold values 0 or 1
Outputs:
- layer_out: bfloat16 [2048, 16384], P('seq', ('row', 'col'))
The draws below stay inside these ranges and needn't reach their ends.
Inputs may be any that keep to these rules, and one draw needn't show every extreme that they name: `block_ids`: block numbers never fall along the sequence; every block holds 1 to 16 tokens and one holds exactly 16.
All inputs are finite; a program needn't handle non-finite values.
Results may differ from the reference program's by a relative error of at most 0.009.
Values may be sent and summed in bfloat16 or wider, within the bound.
No kernel may reach another device: no remote copies, remote signals or barrier semaphores. Data moves between devices by JAX's collectives and lax.ppermute only.
A program may use at most 192 MiB of HBM per device.

```python
import math
import jax
import jax.numpy as jnp
import numpy as np
from jax import lax

D = 16384
HD = 128
QH = 64
KVH = 4
BMAX = 16
LEN = 2048
NBLK = 256


def draw_activations(key, part):
    row_key, col_key, base_key = jax.random.split(key, 3)
    column_ramp = jnp.arange(D, dtype=jnp.float32) / max(D - 1, 1)
    col_scale = jnp.exp(jax.random.uniform(col_key, (1, D), dtype=jnp.float32) * math.log(10.0) + math.log(3.0) * column_ramp[None, :])
    row_scale = jnp.exp(jax.random.uniform(row_key, (LEN, 1), dtype=jnp.float32) * math.log(10.0))
    base_draw = jax.random.truncated_normal(base_key, -4.0, 4.0, (LEN, D), dtype=jnp.float32)
    return (base_draw * row_scale * col_scale).astype(jnp.bfloat16)


def touch_ends(entries, rng, low, high):
    shape = entries.shape
    place = [jax.random.randint(jax.random.fold_in(rng, axis), (), 0, shape[axis]) for axis in range(len(shape))]
    entries = entries.at[tuple(place)].set(low)
    longest = shape.index(max(shape))
    place[longest] = (place[longest] + 1) % shape[longest]
    return entries.at[tuple(place)].set(high)


def levels(rng, dims, cuts, low, top_value):
    loudness, own = 1.0, jax.random.fold_in(rng, 6)
    for dim, shards_of in cuts:
        draws = jnp.exp(jax.random.uniform(jax.random.fold_in(own, dim), (shards_of,), jnp.float32, low / len(cuts), top_value / len(cuts)))
        loudness = loudness * jnp.repeat(draws, dims[dim] // shards_of).reshape([-1 if axis == dim else 1 for axis in range(len(dims))])
    return loudness


def length_profile(amount, total, most, lean):
    portions = [(1 << 20) // math.isqrt(rank ** lean) + 1 for rank in range(2, amount + 1)]
    surplus, counts = total - most - (amount - 1), [1] * (amount - 1)
    while surplus > 0:
        free = [i for i in range(amount - 1) if counts[i] < most]
        whole, remaining = sum([portions[i] for i in free]), surplus
        for i in free:
            addition = min(most - counts[i], max(1, remaining * portions[i] // whole), surplus)
            counts[i] = counts[i] + addition
            surplus = surplus - addition
    return np.array([most] + counts)


def ragged(own_key, number_of, total, bound, skew):
    if number_of == 2:
        one = jax.random.randint(own_key, (), max(1, total - bound), min(bound, total - 1) + 1)
        return jnp.stack([one, total - one])
    sizes = jnp.asarray(length_profile(number_of, total, bound, skew), jnp.int32)
    pairs = (number_of - 1) // 2
    source_of, receiver = sizes[1:1 + 2 * pairs:2], sizes[2:2 + 2 * pairs:2]
    margin = jnp.minimum(source_of - 1, bound - receiver)
    passed = jax.random.randint(jax.random.fold_in(own_key, 1), (pairs,), 0, 1 << 20) % (margin + 1)
    sizes = sizes.at[1:1 + 2 * pairs:2].set(source_of - passed).at[2:2 + 2 * pairs:2].set(receiver + passed)
    return sizes[jax.random.permutation(jax.random.fold_in(own_key, 2), number_of)]


def centred(rng, extent, scale, bound, cuts=(), kind=jnp.bfloat16):
    values = scale * jax.random.normal(rng, extent, jnp.float32)
    if cuts:
        values = values * levels(rng, extent, cuts, -0.22, 0.18)
    return jnp.clip(values, -bound, bound).astype(kind)


def setup_inputs(seed: int = 0) -> dict:
    keys = jax.random.split(jax.random.key(seed), 8)
    activations = draw_activations(jax.random.fold_in(keys[7], 71), 0)
    norm_gain = jnp.clip(1.0 + 0.18 * jax.random.normal(keys[1], (D,), jnp.float32), 0.1, 1.9)
    query_weight = centred(keys[2], (D, QH * HD), D ** -0.5, 0.046875, ((0, 2), (1, 4)))
    kv_weight = centred(keys[3], (D, 2, KVH * HD), D ** -0.5, 0.046875, ((0, 2),))
    out_weight = centred(keys[4], (QH * HD, D), HD ** -0.5, 0.5, ((0, 4), (1, 2)))
    block_ids = jnp.searchsorted(jnp.cumsum(ragged(keys[5], NBLK, LEN, BMAX, 1)), jnp.arange(LEN), side="right").astype(jnp.int32)
    clean_mask = touch_ends((jax.random.randint(keys[6], (LEN,), 0, 2) < 1).astype(jnp.int32), jax.random.fold_in(keys[6], 1), 0, 1)
    return {"activations": activations, "norm_gain": norm_gain, "query_weight": query_weight, "kv_weight": kv_weight, "out_weight": out_weight, "block_ids": block_ids, "clean_mask": clean_mask}


rope_base = 500000.0
norm_eps = 1e-05

def rotate(values, positions):
    half_dim = values.shape[-1] // 2
    inverse = jnp.exp(jnp.arange(half_dim, dtype=jnp.float32) * (-2.0 * math.log(rope_base) / values.shape[-1]))
    angles = positions.astype(jnp.float32)[:, None] * inverse[None, :]
    cosine = jnp.cos(angles)
    sine_part = jnp.sin(angles)
    first_half = values[..., :half_dim]
    second_half = values[..., half_dim:]
    return jnp.concatenate([first_half * cosine - second_half * sine_part, second_half * cosine + first_half * sine_part], axis=-1)

def reference(activations, norm_gain, query_weight, kv_weight, out_weight, block_ids, clean_mask):
    wide_input = activations.astype(jnp.float32)
    scaling = lax.rsqrt(lax.optimization_barrier(jnp.sum(wide_input * wide_input, axis=1)) / D + norm_eps)
    normed = (wide_input * scaling[:, None] * norm_gain[None, :]).astype(jnp.bfloat16)
    positions = jnp.arange(LEN, dtype=jnp.int32)
    query_raw = jnp.dot(normed, query_weight, preferred_element_type=jnp.float32).reshape(LEN, QH, HD).transpose(1, 0, 2)
    queries = rotate(query_raw, positions).astype(jnp.bfloat16)
    kv_raw = jnp.dot(normed, kv_weight.reshape(D, 2 * KVH * HD), preferred_element_type=jnp.float32).reshape(LEN, 2, KVH, HD)
    key_rows = rotate(kv_raw[:, 0].transpose(1, 0, 2), positions).astype(jnp.bfloat16)
    value_rows = kv_raw[:, 1].transpose(1, 0, 2).astype(jnp.bfloat16)
    own_block = block_ids[:, None]
    key_block = block_ids[None, :]
    visible = (key_block == own_block) | (key_block < own_block) & (clean_mask[None, :] == 1)
    group_size = QH // KVH
    score_scale = 1.0 / math.sqrt(HD)

    def one_head(head_index):
        query_head = lax.dynamic_index_in_dim(queries, head_index, 0, keepdims=False)
        kv_index = head_index // group_size
        key_head = lax.dynamic_index_in_dim(key_rows, kv_index, 0, keepdims=False)
        value_head = lax.dynamic_index_in_dim(value_rows, kv_index, 0, keepdims=False)
        scores = jnp.dot(query_head, key_head.T, preferred_element_type=jnp.float32) * score_scale
        weights = jnp.where(visible, jnp.exp(scores), jnp.zeros_like(scores))
        totals = lax.optimization_barrier(jnp.sum(weights, axis=1))
        summed = jnp.dot(weights.astype(jnp.bfloat16), value_head, preferred_element_type=jnp.float32)
        return (summed / totals[:, None]).astype(jnp.bfloat16)
    attended = lax.map(one_head, jnp.arange(QH, dtype=jnp.int32))
    merged = attended.transpose(1, 0, 2).reshape(LEN, QH * HD)
    return jnp.dot(merged, out_weight, preferred_element_type=jnp.float32).astype(jnp.bfloat16)
```

```python
import functools
import math

import jax
import jax.numpy as jnp
from jax import lax
from jax.experimental import pallas as pl
from jax.experimental.pallas import tpu as pltpu
from jax.sharding import PartitionSpec as P

D = 16384
HD = 128
QH = 64
KVH = 4


rope_base = 500000.0
norm_eps = 1e-05


def rotate(values, positions):
    half_dim = values.shape[-1] // 2
    inverse = jnp.exp(
        jnp.arange(half_dim, dtype=jnp.float32) * (-2.0 * math.log(rope_base) / values.shape[-1])
    )
    angles = positions.astype(jnp.float32)[:, None] * inverse[None, :]
    cosine = jnp.cos(angles)
    sine_part = jnp.sin(angles)
    first_half = values[..., :half_dim]
    second_half = values[..., half_dim:]
    return jnp.concatenate(
        [
            first_half * cosine - second_half * sine_part,
            second_half * cosine + first_half * sine_part,
        ],
        axis=-1,
    )


def gathered_shards(activations, norm_gain, query_weight, kv_weight, out_weight, block_ids, clean_mask):
    row_count = lax.axis_size("row")
    col_index = lax.axis_index("col")
    seq_index = lax.axis_index("seq")
    slab_len = activations.shape[0]
    col_heads = query_weight.shape[1] // HD
    dev_heads = col_heads // row_count
    group_size = QH // KVH
    wide_input = activations.astype(jnp.float32)
    squares = lax.psum(jnp.sum(wide_input * wide_input, axis=1), ("row", "col"))
    scaling = lax.rsqrt(squares / D + norm_eps)
    normed = (wide_input * scaling[:, None] * norm_gain[None, :]).astype(jnp.bfloat16)
    panel_rows = lax.all_gather(normed, "col", axis=1, tiled=True)
    kv_count = max(col_heads // group_size, 1)
    kv_first = col_index * col_heads // group_size
    kv_tiles = lax.dynamic_slice_in_dim(kv_weight, kv_first * HD, kv_count * HD, 2)
    kv_term = jnp.einsum("td,dke->kte", panel_rows, kv_tiles, preferred_element_type=jnp.float32)
    columns = query_weight
    columns = columns.reshape(columns.shape[0], dev_heads * lax.axis_size("row"), HD)
    query_sum = lax.psum_scatter(
        jnp.einsum("td,dhe->hte", panel_rows, columns, preferred_element_type=jnp.float32),
        "row",
        scatter_dimension=0,
        tiled=True,
    )
    kv_sum = lax.psum(kv_term, "row")
    key_raw = kv_sum[0]
    value_rows = kv_sum[1].astype(jnp.bfloat16)
    positions = seq_index * slab_len + jnp.arange(slab_len, dtype=jnp.int32)
    key_rows = rotate(key_raw, positions).astype(jnp.bfloat16)
    queries = rotate(query_sum, positions).astype(jnp.bfloat16)
    my_blocks = lax.dynamic_slice_in_dim(block_ids, seq_index * slab_len, slab_len, 0)
    score_scale = 1.0 / math.sqrt(HD)
    key_piece = lax.all_gather(key_rows, "seq", axis=0, tiled=True)
    value_piece = lax.all_gather(value_rows, "seq", axis=0, tiled=True)
    visible = (block_ids[None, :] == my_blocks[:, None]) | (
        block_ids[None, :] < my_blocks[:, None]
    ) & (clean_mask[None, :] == 1)
    scores = (
        jnp.einsum("hte,ne->htn", queries, key_piece, preferred_element_type=jnp.float32)
        * score_scale
    )
    weights = jnp.where(visible[None, :, :], jnp.exp(scores), jnp.zeros_like(scores))
    numerator = jnp.einsum(
        "htn,ne->hte", weights.astype(jnp.bfloat16), value_piece, preferred_element_type=jnp.float32
    )
    denominator = jnp.sum(weights, axis=2)
    numerator, denominator = (numerator, denominator)
    attended = (numerator / denominator[:, :, None]).astype(jnp.bfloat16)
    out_cols = out_weight.shape[1]
    portion = lax.all_gather(attended, "row", axis=0, tiled=True)
    heads_here = portion.shape[0]
    out_rows = out_weight
    out_rows = out_rows.reshape(heads_here, HD, out_cols)
    partial_out = jnp.einsum("hte,hed->td", portion, out_rows, preferred_element_type=jnp.float32)
    projected = lax.psum_scatter(partial_out, "col", scatter_dimension=1, tiled=True)
    return projected.astype(jnp.bfloat16)


LINE = 4
OUTER_IN = ((0, 1), (3, 2))
OUTER_OUT = ((2, 3), (1, 0))
MIDDLE = ((1, 2), (2, 1))
DEST_ORDER = ((3, 2, 1, 0), (0, 3, 2, 1), (3, 0, 1, 2), (0, 1, 2, 3))
FEATURE_ORDER = ((0, 1, 2, 3), (1, 0, 2, 3), (2, 3, 1, 0), (3, 2, 1, 0))
CHUNKS = 4
DEPTH = 512


def hop(values, pairs, axis="col"):
    return lax.ppermute(values, axis, list(pairs))


def params(mib=40):
    return pltpu.CompilerParams(vmem_limit_bytes=mib << 20)


def fetch_features(meta_ref, slots, features, held, arrived, start):
    for place, choices in enumerate(slots):
        def act(which):
            copy = pltpu.make_async_copy(features[which], held.at[place], arrived.at[place])
            copy.start() if start else copy.wait()

        if len(choices) == 1:
            act(choices[0])
        else:
            pl.when(meta_ref[4] == 0)(functools.partial(act, choices[0]))
            pl.when(meta_ref[4] == 1)(functools.partial(act, choices[1]))


def project_first_kernel(slots, meta_ref, *refs):
    count = max(max(choices) for choices in slots) + 1
    features, (weight_ref, total_ref, held, arrived) = refs[:count], refs[count:]
    slot, step = pl.program_id(0), pl.program_id(1)

    @pl.when((slot == 0) & (step == 0))
    def _():
        fetch_features(meta_ref, slots, features, held, arrived, True)

    for place in range(len(slots)):
        @pl.when((slot == place) & (step == 0))
        def _():
            pltpu.make_async_copy(features[0], held.at[place], arrived.at[place]).wait()

    part = jnp.dot(
        held[slot, :, pl.ds(pl.multiple_of(step * DEPTH, DEPTH), DEPTH)],
        weight_ref[...],
        preferred_element_type=jnp.float32,
    )

    @pl.when((slot == 0) & (step == 0))
    def _():
        total_ref[...] = part

    @pl.when((slot > 0) | (step > 0))
    def _():
        total_ref[...] += part


def project_first(meta, slots, features, weight):
    rows, width = features[0].shape
    steps = width // DEPTH
    columns = weight.shape[1]
    return pl.pallas_call(
        functools.partial(project_first_kernel, slots),
        grid_spec=pltpu.PrefetchScalarGridSpec(
            num_scalar_prefetch=1,
            grid=(len(slots), steps),
            in_specs=[pl.BlockSpec(memory_space=pl.ANY)] * len(features)
            + [pl.BlockSpec((DEPTH, columns), lambda i, j, m: (m[i] * steps + j, 0))],
            out_specs=pl.BlockSpec((rows, columns), lambda i, j, m: (0, 0)),
            scratch_shapes=[
                pltpu.VMEM((len(slots), rows, width), jnp.bfloat16),
                pltpu.SemaphoreType.DMA((len(slots),)),
            ],
        ),
        out_shape=jax.ShapeDtypeStruct((rows, columns), jnp.float32),
        compiler_params=params(),
        cost_estimate=pl.CostEstimate(
            flops=2 * rows * width * columns * len(slots),
            bytes_accessed=2 * width * columns * len(slots),
            transcendentals=0,
        ),
        name="project_first",
    )(meta, *features, weight)


def project_last_kernel(meta_ref, middle_ref, end_ref, weight_ref, so_far_ref, mine_ref, other_ref, held, total, arrived):
    step = pl.program_id(0)
    half = mine_ref.shape[1]

    @pl.when(step == 0)
    def _():
        fetch_features(meta_ref, ((0, 1),), (middle_ref, end_ref), held, arrived, True)
        total[...] = so_far_ref[...]
        pltpu.make_async_copy(middle_ref, held.at[0], arrived.at[0]).wait()

    total[...] += jnp.dot(
        held[0, :, pl.ds(pl.multiple_of(step * DEPTH, DEPTH), DEPTH)],
        weight_ref[...],
        preferred_element_type=jnp.float32,
    )

    @pl.when(step == pl.num_programs(0) - 1)
    def _():
        mine = meta_ref[5]
        mine_ref[...] = total[:, pl.ds(pl.multiple_of(mine * half, half), half)]
        other_ref[...] = total[:, pl.ds(pl.multiple_of((1 - mine) * half, half), half)]


def project_last(meta, middle, end, weight, so_far):
    rows, width = middle.shape
    steps = width // DEPTH
    columns = weight.shape[1]
    whole = lambda i, m: (0, 0)
    return pl.pallas_call(
        project_last_kernel,
        grid_spec=pltpu.PrefetchScalarGridSpec(
            num_scalar_prefetch=1,
            grid=(steps,),
            in_specs=[
                pl.BlockSpec(memory_space=pl.ANY),
                pl.BlockSpec(memory_space=pl.ANY),
                pl.BlockSpec((DEPTH, columns), lambda i, m: (m[3] * steps + i, 0)),
                pl.BlockSpec((rows, columns), whole),
            ],
            out_specs=[pl.BlockSpec((rows, columns // 2), whole)] * 2,
            scratch_shapes=[
                pltpu.VMEM((1, rows, width), jnp.bfloat16),
                pltpu.VMEM((rows, columns), jnp.float32),
                pltpu.SemaphoreType.DMA((1,)),
            ],
        ),
        out_shape=[jax.ShapeDtypeStruct((rows, columns // 2), jnp.float32)] * 2,
        compiler_params=params(),
        cost_estimate=pl.CostEstimate(
            flops=2 * rows * width * columns, bytes_accessed=2 * width * columns, transcendentals=0
        ),
        name="project_last",
    )(meta, middle, end, weight, so_far)


def attend_kernel(
    mine_ref, arrived_ref, cosine_ref, sine_ref, key_ref, value_ref, own_ids_ref, ids_ref, cut_ref, out_ref, bias
):
    rows = mine_ref.shape[0]
    keys = key_ref.shape[0]
    tile = min(512, keys)
    own = own_ids_ref[...]
    for first in range(0, keys, tile):
        spot = slice(first, first + tile)
        seen = (ids_ref[:, spot] == own) | (cut_ref[:, spot] < own)
        bias[:, spot] = jnp.where(seen, 0.0, -jnp.inf)
    factor = math.log2(math.e) / math.sqrt(HD)

    def one_head(head, carry):
        place = pl.ds(pl.multiple_of(head * HD, HD), HD)
        raw = mine_ref[:, place] + arrived_ref[:, place]
        query = (raw * cosine_ref[...] + pltpu.roll(raw, HD // 2, 1) * sine_ref[...]).astype(jnp.bfloat16)
        summed = jnp.zeros((rows, value_ref.shape[1]), jnp.float32)
        for first in range(0, keys, tile):
            spot = slice(first, first + tile)
            scores = lax.dot_general(
                query, key_ref[spot, :], (((1,), (1,)), ((), ())), preferred_element_type=jnp.float32
            )
            weights = jnp.exp2(scores * factor + bias[:, spot])
            summed += jnp.dot(weights.astype(jnp.bfloat16), value_ref[spot, :], preferred_element_type=jnp.float32)
        out_ref[:, place] = (summed[:, :HD] / summed[:, HD:]).astype(jnp.bfloat16)
        return carry

    lax.fori_loop(0, mine_ref.shape[1] // HD, one_head, 0)


def attend(mine, arrived, cosine, sine, keys, values, own_ids, ids, cut):
    rows, width = mine.shape
    return pl.pallas_call(
        attend_kernel,
        out_shape=jax.ShapeDtypeStruct((rows, width), jnp.bfloat16),
        in_specs=[pl.BlockSpec(memory_space=pltpu.VMEM)] * 9,
        out_specs=pl.BlockSpec(memory_space=pltpu.VMEM),
        scratch_shapes=[pltpu.VMEM((rows, keys.shape[0]), jnp.float32)],
        compiler_params=params(),
        cost_estimate=pl.CostEstimate(
            flops=8 * rows * keys.shape[0] * width,
            bytes_accessed=8 * rows * width + 6 * keys.shape[0] * HD,
            transcendentals=rows * keys.shape[0] * width // HD,
        ),
        name="attend",
    )(mine, arrived, cosine, sine, keys, values, own_ids, ids, cut)


def output_kernel(meta_ref, mine_ref, other_ref, weight_ref, first_ref, second_ref, total):
    slot, step = pl.program_id(0), pl.program_id(1)
    steps = pl.num_programs(1)
    near = steps // 2
    place = pl.ds(pl.multiple_of(lax.rem(step, near) * DEPTH, DEPTH), DEPTH)

    @pl.when(step < near)
    def _():
        part = jnp.dot(mine_ref[:, place], weight_ref[...], preferred_element_type=jnp.float32)

        @pl.when(step == 0)
        def _():
            total[...] = part

        @pl.when(step > 0)
        def _():
            total[...] += part

    @pl.when(step >= near)
    def _():
        total[...] += jnp.dot(other_ref[:, place], weight_ref[...], preferred_element_type=jnp.float32)

    @pl.when((step == steps - 1) & (slot == 0))
    def _():
        first_ref[...] = total[...].astype(first_ref.dtype)

    @pl.when((step == steps - 1) & (slot == 1))
    def _():
        second_ref[...] = total[...].astype(second_ref.dtype)


def output_parts(meta, first_slot, mine, other, weight, kinds):
    rows, width = mine.shape
    steps = weight.shape[0] // DEPTH
    near = steps // 2
    columns = weight.shape[1] // LINE
    whole = lambda i, j, m: (0, 0)

    def weight_block(i, j, m):
        return (lax.rem(j + m[5] * near, steps), m[6 + first_slot + i])

    return pl.pallas_call(
        output_kernel,
        grid_spec=pltpu.PrefetchScalarGridSpec(
            num_scalar_prefetch=1,
            grid=(2, steps),
            in_specs=[pl.BlockSpec((rows, width), whole)] * 2 + [pl.BlockSpec((DEPTH, columns), weight_block)],
            out_specs=[pl.BlockSpec((rows, columns), whole)] * 2,
            scratch_shapes=[pltpu.VMEM((rows, columns), jnp.float32)],
        ),
        out_shape=[jax.ShapeDtypeStruct((rows, columns), kind) for kind in kinds],
        compiler_params=params(),
        cost_estimate=pl.CostEstimate(
            flops=8 * rows * width * columns, bytes_accessed=8 * width * columns, transcendentals=0
        ),
        name="output_parts",
    )(meta, mine, other, weight)


def line_shards(activations, norm_gain, query_weight, kv_weight, out_weight, block_ids, clean_mask):
    col, row, seq = (lax.axis_index(axis) for axis in ("col", "row", "seq"))
    slab, width = activations.shape
    rows = slab // CHUNKS
    half = slab // 2
    swap = ((0, 1), (1, 0))
    at_end = (col == 0) | (col == LINE - 1)
    meta = jnp.concatenate(
        [
            jnp.asarray(FEATURE_ORDER, jnp.int32)[col],
            jnp.stack([at_end.astype(jnp.int32), row.astype(jnp.int32)]),
            jnp.asarray(DEST_ORDER, jnp.int32)[col],
        ]
    )

    wide_input = activations.astype(jnp.float32)
    gained = [
        (wide_input[i * rows : (i + 1) * rows] * norm_gain[None, :]).astype(jnp.bfloat16) for i in range(CHUNKS)
    ]
    gathered = []
    for own in gained:
        beside = hop(own, OUTER_IN + OUTER_OUT)
        across = hop(own, MIDDLE)
        far_middle = hop(beside, MIDDLE)
        far_end = hop(across, OUTER_OUT)
        farthest = hop(far_middle, OUTER_OUT)
        gathered.append((own, beside, across, far_end, far_middle, farthest))

    squares = lax.psum(jnp.sum(wide_input * wide_input, axis=1), ("row", "col"))
    scaling = lax.rsqrt(squares / D + norm_eps)
    inverse = jnp.exp(jnp.arange(HD // 2, dtype=jnp.float32) * (-2.0 * math.log(rope_base) / HD))
    positions = seq * slab + jnp.arange(slab, dtype=jnp.int32)
    angles = positions.astype(jnp.float32)[:, None] * inverse[None, :]
    cosine = jnp.concatenate([jnp.cos(angles)] * 2, axis=1) * scaling[:, None]
    sine = jnp.concatenate([-jnp.sin(angles), jnp.sin(angles)], axis=1) * scaling[:, None]

    local_weight = lax.dynamic_slice_in_dim(kv_weight, col * width, width, 0)
    local_input = (wide_input * norm_gain[None, :]).astype(jnp.bfloat16)
    term = jnp.einsum("td,dke->kte", local_input, local_weight, preferred_element_type=jnp.float32)
    kept = lax.dynamic_slice_in_dim(term, row * half, half, 1)
    given = lax.dynamic_slice_in_dim(term, (1 - row) * half, half, 1)
    both = (kept + hop(given, swap, "row")).astype(jnp.bfloat16)
    kv_sum = lax.dynamic_slice_in_dim(both, col * HD, HD, 2).astype(jnp.float32)
    for offset in range(1, LINE):
        share = lax.dynamic_slice_in_dim(both, (col + offset) % LINE * HD, HD, 2)
        kv_sum += hop(share, [(i, (i + offset) % LINE) for i in range(LINE)]).astype(jnp.float32)
    my_cosine = lax.dynamic_slice_in_dim(cosine, row * half, half, 0)
    my_sine = lax.dynamic_slice_in_dim(sine, row * half, half, 0)
    my_scaling = lax.dynamic_slice_in_dim(scaling, row * half, half, 0)
    turned = jnp.concatenate([kv_sum[0, :, HD // 2 :], kv_sum[0, :, : HD // 2]], axis=1)
    key_rows = (kv_sum[0] * my_cosine + turned * my_sine).astype(jnp.bfloat16)
    value_rows = (kv_sum[1] * my_scaling[:, None]).astype(jnp.bfloat16)
    spread = lax.all_gather(jnp.stack([key_rows, value_rows]), ("seq", "row"), axis=0)
    keys = spread[:, 0].reshape(-1, HD)
    values = spread[:, 1].reshape(-1, HD)
    values = jnp.concatenate([values, jnp.ones_like(values)], axis=1)

    ids = block_ids[None, :]
    cut = jnp.where(clean_mask == 1, block_ids, jnp.iinfo(jnp.int32).max)[None, :]
    my_ids = lax.dynamic_slice_in_dim(block_ids, seq * slab, slab, 0)[:, None]

    out = []
    for i, (own, beside, across, far_end, far_middle, farthest) in enumerate(gathered):
        spot = slice(i * rows, (i + 1) * rows)
        so_far = project_first(meta, ((0,), (1,), (2, 3)), (own, beside, across, far_end), query_weight)
        mine, other = project_last(meta, far_middle, farthest, query_weight, so_far)
        attended = attend(
            mine, hop(other, swap, "row"), cosine[spot], sine[spot], keys, values, my_ids[spot], ids, cut
        )
        other_attended = hop(attended, swap, "row")
        parts = output_parts(meta, 0, attended, other_attended, out_weight, (jnp.bfloat16, jnp.bfloat16))
        parts += output_parts(meta, 2, attended, other_attended, out_weight, (jnp.bfloat16, jnp.float32))
        inward = hop(parts[0], OUTER_IN)
        inward_next = hop(parts[1], OUTER_IN)
        through = hop(parts[1] + inward, MIDDLE)
        last_outer = hop(jnp.where(at_end, parts[2], parts[0] + through), OUTER_IN + OUTER_OUT)
        last_middle = hop(parts[2] + inward_next, MIDDLE)
        out.append(
            (parts[3] + last_outer.astype(jnp.float32) + last_middle.astype(jnp.float32)).astype(jnp.bfloat16)
        )
    return jnp.concatenate(out, axis=0)


def solution(mesh):
    placed = (
        P("seq", ("row", "col")),
        P(("row", "col")),
        P("row", "col"),
        P("row", None, None),
        P("col", "row"),
        P(),
        P(),
    )
    on_line = mesh.shape["col"] == LINE == KVH and mesh.shape["row"] == 2
    return jax.shard_map(
        line_shards if on_line else gathered_shards,
        mesh=mesh,
        in_specs=placed,
        out_specs=P("seq", ("row", "col")),
        check_vma=False,
    )
```

```python
import functools
import math

import jax
import jax.numpy as jnp
from jax import lax
from jax.experimental import pallas as pl
from jax.experimental.pallas import tpu as pltpu
from jax.sharding import PartitionSpec as P

D = 16384
HD = 128
QH = 64
KVH = 4


rope_base = 500000.0
norm_eps = 1e-05


def rotate(values, positions):
    half_dim = values.shape[-1] // 2
    inverse = jnp.exp(
        jnp.arange(half_dim, dtype=jnp.float32) * (-2.0 * math.log(rope_base) / values.shape[-1])
    )
    angles = positions.astype(jnp.float32)[:, None] * inverse[None, :]
    cosine = jnp.cos(angles)
    sine_part = jnp.sin(angles)
    first_half = values[..., :half_dim]
    second_half = values[..., half_dim:]
    return jnp.concatenate(
        [
            first_half * cosine - second_half * sine_part,
            second_half * cosine + first_half * sine_part,
        ],
        axis=-1,
    )


def gathered_shards(activations, norm_gain, query_weight, kv_weight, out_weight, block_ids, clean_mask):
    row_count = lax.axis_size("row")
    col_index = lax.axis_index("col")
    seq_index = lax.axis_index("seq")
    slab_len = activations.shape[0]
    col_heads = query_weight.shape[1] // HD
    dev_heads = col_heads // row_count
    group_size = QH // KVH
    wide_input = activations.astype(jnp.float32)
    squares = lax.psum(jnp.sum(wide_input * wide_input, axis=1), ("row", "col"))
    scaling = lax.rsqrt(squares / D + norm_eps)
    normed = (wide_input * scaling[:, None] * norm_gain[None, :]).astype(jnp.bfloat16)
    panel_rows = lax.all_gather(normed, "col", axis=1, tiled=True)
    kv_count = max(col_heads // group_size, 1)
    kv_first = col_index * col_heads // group_size
    kv_tiles = lax.dynamic_slice_in_dim(kv_weight, kv_first * HD, kv_count * HD, 2)
    kv_term = jnp.einsum("td,dke->kte", panel_rows, kv_tiles, preferred_element_type=jnp.float32)
    columns = query_weight
    columns = columns.reshape(columns.shape[0], dev_heads * lax.axis_size("row"), HD)
    query_sum = lax.psum_scatter(
        jnp.einsum("td,dhe->hte", panel_rows, columns, preferred_element_type=jnp.float32),
        "row",
        scatter_dimension=0,
        tiled=True,
    )
    kv_sum = lax.psum(kv_term, "row")
    key_raw = kv_sum[0]
    value_rows = kv_sum[1].astype(jnp.bfloat16)
    positions = seq_index * slab_len + jnp.arange(slab_len, dtype=jnp.int32)
    key_rows = rotate(key_raw, positions).astype(jnp.bfloat16)
    queries = rotate(query_sum, positions).astype(jnp.bfloat16)
    my_blocks = lax.dynamic_slice_in_dim(block_ids, seq_index * slab_len, slab_len, 0)
    score_scale = 1.0 / math.sqrt(HD)
    key_piece = lax.all_gather(key_rows, "seq", axis=0, tiled=True)
    value_piece = lax.all_gather(value_rows, "seq", axis=0, tiled=True)
    visible = (block_ids[None, :] == my_blocks[:, None]) | (
        block_ids[None, :] < my_blocks[:, None]
    ) & (clean_mask[None, :] == 1)
    scores = (
        jnp.einsum("hte,ne->htn", queries, key_piece, preferred_element_type=jnp.float32)
        * score_scale
    )
    weights = jnp.where(visible[None, :, :], jnp.exp(scores), jnp.zeros_like(scores))
    numerator = jnp.einsum(
        "htn,ne->hte", weights.astype(jnp.bfloat16), value_piece, preferred_element_type=jnp.float32
    )
    denominator = jnp.sum(weights, axis=2)
    numerator, denominator = (numerator, denominator)
    attended = (numerator / denominator[:, :, None]).astype(jnp.bfloat16)
    out_cols = out_weight.shape[1]
    portion = lax.all_gather(attended, "row", axis=0, tiled=True)
    heads_here = portion.shape[0]
    out_rows = out_weight
    out_rows = out_rows.reshape(heads_here, HD, out_cols)
    partial_out = jnp.einsum("hte,hed->td", portion, out_rows, preferred_element_type=jnp.float32)
    projected = lax.psum_scatter(partial_out, "col", scatter_dimension=1, tiled=True)
    return projected.astype(jnp.bfloat16)


LINE = 4
OUTER_IN = ((0, 1), (3, 2))
OUTER_OUT = ((2, 3), (1, 0))
MIDDLE = ((1, 2), (2, 1))
DEST_ORDER = ((3, 2, 1, 0), (0, 3, 2, 1), (3, 0, 1, 2), (0, 1, 2, 3))
FEATURE_ORDER = ((0, 1, 2, 3), (1, 0, 2, 3), (2, 3, 1, 0), (3, 2, 1, 0))
CHUNK_SHARES = (12, 12, 8)
DEPTH = 512
BUFFERS = 4
COST_SCALE = 1.0
EXTRA = 16


def hop(values, pairs, axis="col"):
    return lax.ppermute(values, axis, list(pairs))


def chunk_bounds(slab):
    whole = sum(CHUNK_SHARES)
    marks = [slab * sum(CHUNK_SHARES[:i]) // whole // 16 * 16 for i in range(len(CHUNK_SHARES))] + [slab]
    return list(zip(marks[:-1], marks[1:]))


class Order:
    def __init__(self):
        self.token = []

    def call(self, body, outs, scratch, inputs, spaces, name, out_spaces=None, aliases=None, cost=1_000_000):
        count, given = len(inputs), len(outs)
        tokens = list(self.token)

        def kernel(*refs):
            refs = refs[:count] + refs[count + len(tokens) :]
            body(*refs[: count + given], *refs[count + given + 1 :])

        results = pl.pallas_call(
            kernel,
            out_shape=list(outs) + [jax.ShapeDtypeStruct((8, HD), jnp.float32)],
            in_specs=[pl.BlockSpec(memory_space=space) for space in spaces]
            + [pl.BlockSpec(memory_space=pl.ANY)] * len(tokens),
            out_specs=[pl.BlockSpec(memory_space=space) for space in (out_spaces or [pltpu.VMEM] * given)]
            + [pl.BlockSpec(memory_space=pl.ANY)],
            scratch_shapes=scratch,
            input_output_aliases=aliases or {},
            compiler_params=pltpu.CompilerParams(vmem_limit_bytes=36 << 20),
            cost_estimate=pl.CostEstimate(flops=0, bytes_accessed=int(cost * COST_SCALE), transcendentals=0),
            name=name,
        )(*inputs, *tokens)
        self.token = [results[-1]]
        return results[:-1]

    def arrive(self, *arrays):
        def body(*refs):
            pass

        outs = [jax.ShapeDtypeStruct(array.shape, array.dtype) for array in arrays]
        spaces = [pl.ANY] * len(arrays)
        return self.call(body, outs, [], arrays, spaces, "arrive", spaces, {i: i for i in range(len(arrays))}, 0)

    def add(self, groups, kinds):
        flat = [array for group in groups for array in group]

        def body(*refs):
            ins, outs = refs[: len(flat)], refs[len(flat) :]
            for group, out in zip(groups, outs):
                part, ins = ins[: len(group)], ins[len(group) :]
                out[...] = sum(ref[...].astype(jnp.float32) for ref in part).astype(out.dtype)

        outs = [jax.ShapeDtypeStruct(group[0].shape, kind) for group, kind in zip(groups, kinds)]
        return self.call(body, outs, [], flat, [pltpu.VMEM] * len(flat), "adding")


def last_sums(order, meta, first, third, fourth, through, inward_next):
    def body(meta_ref, first_ref, third_ref, through_ref, next_ref, outer, middle):
        @pl.when(meta_ref[4] == 1)
        def _():
            outer[...] = third_ref[...]

        @pl.when(meta_ref[4] == 0)
        def _():
            wide = first_ref[...].astype(jnp.float32) + through_ref[...].astype(jnp.float32)
            outer[...] = wide.astype(outer.dtype)

        wide = third_ref[...].astype(jnp.float32) + next_ref[...].astype(jnp.float32)
        middle[...] = wide.astype(middle.dtype)

    outer, middle = order.call(
        body,
        [jax.ShapeDtypeStruct(first.shape, first.dtype)] * 2,
        [],
        [meta, first, third, through, inward_next],
        [pltpu.SMEM] + [pltpu.VMEM] * 4,
        "last_sums",
    )
    return fourth, outer, middle


def gain_rows(order, activations, gain, rows):
    width = activations.shape[1]

    def body(source, gain_ref, out, held, here):
        copy = pltpu.make_async_copy(source.at[:rows, :], held, here)
        copy.start()
        copy.wait()
        out[...] = (held[...].astype(jnp.float32) * gain_ref[...]).astype(out.dtype)

    return order.call(
        body,
        [jax.ShapeDtypeStruct((rows, width), jnp.bfloat16)],
        [pltpu.VMEM((rows, width), jnp.bfloat16), pltpu.SemaphoreType.DMA(())],
        [activations, gain],
        [pl.ANY, pltpu.VMEM],
        "gain_rows",
    )[0]


def key_value_terms(order, meta, activations, gain, weight, bounds):
    slab, width = activations.shape
    columns = weight.shape[1] * weight.shape[2]
    half = slab // 2
    steps = width // DEPTH

    def body(meta_ref, source, gain_ref, weight_ref, kept, given, *refs):
        outs, (gained, total, held, buffer, here, arrived) = refs[:-6], refs[-6:]
        brought = pltpu.make_async_copy(source, held, here)
        brought.start()

        def place(step):
            return pl.ds(meta_ref[10] * width + step * DEPTH, DEPTH)

        def multiply(step, block):
            @pl.when(step == 0)
            def _():
                brought.wait()
                wide = held[...].astype(jnp.float32)
                gained[...] = (wide * gain_ref[...]).astype(gained.dtype)
                total[...] = jnp.zeros_like(total)

            left = gained[:, pl.ds(pl.multiple_of(step * DEPTH, DEPTH), DEPTH)]
            total[...] += jnp.dot(left, block.reshape(DEPTH, columns), preferred_element_type=jnp.float32)

        streamed(weight_ref, place, steps, buffer, arrived, multiply)
        wide = held[...].astype(jnp.float32)
        squares = jnp.sum(wide * wide, axis=1, keepdims=True)
        diagonal = lax.broadcasted_iota(jnp.int32, (HD, HD), 0) == lax.broadcasted_iota(jnp.int32, (HD, HD), 1)
        for out, which in ((given, 1 - meta_ref[5]), (kept, meta_ref[5])):
            out[:half, :] = total[pl.ds(pl.multiple_of(which * half, half), half), :]
            out[half:, :] = jnp.zeros((EXTRA, columns), jnp.float32)
            for block in range(slab // HD):
                part = jnp.broadcast_to(squares[block * HD : (block + 1) * HD], (HD, HD))
                out[half : half + 1, block * HD : (block + 1) * HD] = jnp.sum(
                    jnp.where(diagonal, part, 0.0), axis=0, keepdims=True
                )
        for (low, high), out in zip(bounds, outs):
            out[...] = gained[low:high, :]

    kept, given, *gained = order.call(
        body,
        [jax.ShapeDtypeStruct((half + EXTRA, columns), jnp.float32)] * 2
        + [jax.ShapeDtypeStruct((high - low, width), jnp.bfloat16) for low, high in bounds],
        [
            pltpu.VMEM((slab, width), jnp.bfloat16),
            pltpu.VMEM((slab, columns), jnp.float32),
            pltpu.VMEM((slab, width), jnp.bfloat16),
            pltpu.VMEM((BUFFERS, DEPTH) + weight.shape[1:], jnp.bfloat16),
            pltpu.SemaphoreType.DMA(()),
            pltpu.SemaphoreType.DMA((BUFFERS,)),
        ],
        [meta, activations, gain, weight],
        [pltpu.SMEM, pl.ANY, pltpu.VMEM, pl.ANY],
        "key_value_terms",
        cost=15_000_000,
    )
    return kept, given, gained


def key_value_shares(order, meta, kept, arrived):
    rows, columns = kept.shape[0] - EXTRA, kept.shape[1]
    heads = columns // (2 * HD)

    def body(meta_ref, kept_ref, arrived_ref, *outs):
        squares = kept_ref[rows : rows + 1, :] + arrived_ref[rows : rows + 1, :]
        pieces, rest = [], squares
        for _ in range(3):
            piece = rest.astype(jnp.bfloat16)
            pieces.append(piece.astype(jnp.float32))
            rest = rest - pieces[-1]
        blocks = 2 * rows // HD
        lines = [
            jnp.concatenate([piece[:, i * HD : (i + 1) * HD] for piece in (pieces[0], pieces[1])], axis=1)
            for i in range(blocks)
        ] + [
            jnp.concatenate([pieces[2][:, i * HD : (i + 1) * HD]] * 2, axis=1) for i in range(blocks)
        ]
        lines = jnp.concatenate(lines + [jnp.zeros((EXTRA - 2 * blocks, 2 * HD), jnp.float32)], axis=0)
        for offset, out in enumerate(outs):
            head = lax.rem(meta_ref[10] + offset, heads)
            for part in range(2):
                spot = pl.ds(pl.multiple_of(part * heads * HD + head * HD, HD), HD)
                both = kept_ref[:rows, spot] + arrived_ref[:rows, spot]
                out[:rows, part * HD : (part + 1) * HD] = both.astype(out.dtype)
            out[rows:, :] = lines.astype(out.dtype)

    return order.call(
        body,
        [jax.ShapeDtypeStruct((rows + EXTRA, 2 * HD), jnp.float32)]
        + [jax.ShapeDtypeStruct((rows + EXTRA, 2 * HD), jnp.bfloat16)] * (heads - 1),
        [],
        [meta, kept, arrived],
        [pltpu.SMEM, pltpu.VMEM, pltpu.VMEM],
        "key_value_shares",
    )


def key_value_rows(order, meta, shares, cosine, sine):
    rows = shares[0].shape[0] - EXTRA
    blocks = 2 * rows // HD

    def body(meta_ref, *refs):
        share_refs, (cosine_ref, sine_ref, out, cosine_out, sine_out, scaling) = refs[: len(shares)], refs[len(shares) :]
        total = sum(ref[...].astype(jnp.float32) for ref in share_refs)
        diagonal = lax.broadcasted_iota(jnp.int32, (HD, HD), 0) == lax.broadcasted_iota(jnp.int32, (HD, HD), 1)
        for block in range(blocks):
            line = total[rows + block : rows + block + 1, :]
            last = total[rows + blocks + block : rows + blocks + block + 1, :HD]
            squares = line[:, :HD] + line[:, HD:] + last
            factor = lax.rsqrt(squares / D + norm_eps)
            column = jnp.sum(jnp.where(diagonal, factor, 0.0), axis=1, keepdims=True)
            scaling[block * HD : (block + 1) * HD, :] = jnp.broadcast_to(column, (HD, HD))
        cosine_out[...] = cosine_ref[...] * scaling[...]
        sine_out[...] = sine_ref[...] * scaling[...]
        spot = pl.ds(pl.multiple_of(meta_ref[5] * rows, rows), rows)
        raw = total[:rows, :HD]
        turned = pltpu.roll(raw, HD // 2, 1)
        out[:, :HD] = (raw * cosine_out[spot, :] + turned * sine_out[spot, :]).astype(out.dtype)
        out[:, HD:] = (total[:rows, HD:] * scaling[spot, :]).astype(out.dtype)

    inputs = [meta, *shares, cosine, sine]
    return order.call(
        body,
        [jax.ShapeDtypeStruct((rows, 2 * HD), jnp.bfloat16)] + [jax.ShapeDtypeStruct(cosine.shape, jnp.float32)] * 2,
        [pltpu.VMEM(cosine.shape, jnp.float32)],
        inputs,
        [pltpu.SMEM] + [pltpu.VMEM] * (len(inputs) - 1),
        "key_value_rows",
    )


def final_rows(order, so_far, slab, bounds, parts):
    rows, width = parts[0].shape

    def body(*refs):
        ins = refs[: len(parts)]
        out, held, here = refs[-3:]
        held[...] = sum(ref[...].astype(jnp.float32) for ref in ins).astype(held.dtype)
        copy = pltpu.make_async_copy(held, out.at[slice(*bounds), :], here)
        copy.start()
        copy.wait()

    inputs = list(parts) + ([] if so_far is None else [so_far])
    return order.call(
        body,
        [jax.ShapeDtypeStruct((slab, width), jnp.bfloat16)],
        [pltpu.VMEM((rows, width), jnp.bfloat16), pltpu.SemaphoreType.DMA(())],
        inputs,
        [pltpu.VMEM] * len(parts) + [pl.ANY] * (len(inputs) - len(parts)),
        "final_rows",
        [pl.ANY],
        {} if so_far is None else {len(parts): 0},
    )[0]


def streamed(weight_ref, place, steps, buffer, arrived, multiply):
    depth = buffer.shape[0]

    def copy(step):
        spot = lax.rem(step, depth)
        return pltpu.make_async_copy(weight_ref.at[place(step)], buffer.at[spot], arrived.at[spot])

    for step in range(min(depth, steps)):
        copy(jnp.int32(step)).start()

    def one(step, carry):
        copy(step).wait()
        multiply(step, buffer[lax.rem(step, depth)])

        @pl.when(step + depth < steps)
        def _():
            copy(step + depth).start()

        return carry

    lax.fori_loop(0, steps, one, 0)


def project(order, meta, slots, features, so_far, weight, split):
    rows, width = features[0].shape[-2:]
    columns = weight.shape[1]
    steps = width // DEPTH
    first, turns = slots[0][0] if slots else 0, len(slots) or LINE

    def body(meta_ref, weight_ref, *refs):
        if so_far is not None:
            so_far_ref, refs = refs[0], refs[1:]
        feature_refs, refs = refs[: len(features)], refs[len(features) :]
        if split:
            outs, (total, held, buffer, here, arrived) = refs[:-5], refs[-5:]
        else:
            (total,), (held, buffer, here, arrived) = refs[:-4], refs[-4:]
        if so_far is not None:
            brought = pltpu.make_async_copy(so_far_ref, total, here.at[turns])
            brought.start()
        if not slots:
            for turn in range(turns):
                pltpu.make_async_copy(feature_refs[0].at[turn], held.at[turn], here.at[turn]).start()
        for turn, (_, choices) in enumerate(slots):
            def start(which):
                pltpu.make_async_copy(feature_refs[which], held.at[turn], here.at[turn]).start()

            if len(choices) == 1:
                start(choices[0])
            else:
                pl.when(meta_ref[4] == 0)(functools.partial(start, choices[0]))
                pl.when(meta_ref[4] == 1)(functools.partial(start, choices[1]))
        def place(step):
            block = meta_ref[first + step // steps] * steps + lax.rem(step, steps) if slots else step
            return (pl.ds(pl.multiple_of(block * DEPTH, DEPTH), DEPTH), slice(None))

        def multiply(step, block):
            turn, inner = step // steps, lax.rem(step, steps)

            @pl.when(step == 0)
            def _():
                if so_far is None:
                    total[...] = jnp.zeros_like(total)
                else:
                    brought.wait()

            @pl.when(inner == 0)
            def _():
                source = feature_refs[0] if slots else feature_refs[0].at[0]
                pltpu.make_async_copy(source, held.at[turn], here.at[turn]).wait()

            left = held[turn, :, pl.ds(pl.multiple_of(inner * DEPTH, DEPTH), DEPTH)]
            total[...] += jnp.dot(left, block, preferred_element_type=jnp.float32)

        streamed(weight_ref, place, turns * steps, buffer, arrived, multiply)
        if split:
            half = columns // 2
            mine = meta_ref[5]
            outs[0][...] = total[:, pl.ds(pl.multiple_of(mine * half, half), half)]
            outs[1][...] = total[:, pl.ds(pl.multiple_of((1 - mine) * half, half), half)]

    whole = jax.ShapeDtypeStruct((rows, columns), jnp.float32)
    halves = jax.ShapeDtypeStruct((rows, columns // 2), jnp.float32)
    inputs = [meta, weight] + ([] if so_far is None else [so_far]) + list(features)
    spaces = [pltpu.SMEM, pl.ANY] + ([] if so_far is None else [pl.ANY]) + [pl.ANY] * len(features)
    return order.call(
        body,
        [halves, halves] if split else [whole],
        ([pltpu.VMEM((rows, columns), jnp.float32)] if split else [])
        + [
            pltpu.VMEM((turns, rows, width), jnp.bfloat16),
            pltpu.VMEM((BUFFERS, DEPTH, columns), jnp.bfloat16),
            pltpu.SemaphoreType.DMA((turns + 1,)),
            pltpu.SemaphoreType.DMA((BUFFERS,)),
        ],
        inputs,
        spaces,
        "project",
        cost=2 * turns * width * columns,
    )


def attend(order, mine, arrived, bounds, cosine, sine, pairs, own_ids, ids, cut):
    rows, width = mine.shape
    key_count = pairs.shape[0]
    tile = min(512, key_count)
    spot_rows = slice(*bounds)
    factor = math.log2(math.e) / math.sqrt(HD)

    def body(
        mine_ref, arrived_ref, cosine_ref, sine_ref, pair_ref, own_ids_ref, ids_ref, cut_ref, out_ref, bias, values
    ):
        values[:, :HD] = pair_ref[:, HD:]
        values[:, HD:] = jnp.ones((key_count, HD), values.dtype)
        own = own_ids_ref[spot_rows, :1]
        for first in range(0, key_count, tile):
            spot = slice(first, first + tile)
            seen = (ids_ref[:, spot] == own) | (cut_ref[:, spot] < own)
            bias[:, spot] = jnp.where(seen, 0.0, -jnp.inf)

        def one_head(head, carry):
            place = pl.ds(pl.multiple_of(head * HD, HD), HD)
            raw = mine_ref[:, place] + arrived_ref[:, place]
            turned = pltpu.roll(raw, HD // 2, 1)
            query = (raw * cosine_ref[spot_rows, :] + turned * sine_ref[spot_rows, :]).astype(jnp.bfloat16)
            summed = jnp.zeros((rows, values.shape[1]), jnp.float32)
            for first in range(0, key_count, tile):
                spot = slice(first, first + tile)
                scores = lax.dot_general(
                    query, pair_ref[spot, :HD], (((1,), (1,)), ((), ())), preferred_element_type=jnp.float32
                )
                weights = jnp.exp2(scores * factor + bias[:, spot])
                summed += jnp.dot(weights.astype(jnp.bfloat16), values[spot, :], preferred_element_type=jnp.float32)
            out_ref[:, place] = (summed[:, :HD] / summed[:, HD:]).astype(jnp.bfloat16)
            return carry

        lax.fori_loop(0, width // HD, one_head, 0, unroll=2)

    return order.call(
        body,
        [jax.ShapeDtypeStruct((rows, width), jnp.bfloat16)],
        [pltpu.VMEM((rows, key_count), jnp.float32), pltpu.VMEM((key_count, 2 * HD), jnp.bfloat16)],
        [mine, arrived, cosine, sine, pairs, own_ids, ids, cut],
        [pltpu.VMEM] * 8,
        "attend",
        cost=20_000_000,
    )[0]


def output_parts(order, meta, first_slot, mine, other, weight, kinds):
    rows, width = mine.shape
    steps = weight.shape[0] // DEPTH
    near = steps // 2
    columns = weight.shape[1] // LINE
    turns = len(kinds)

    def body(meta_ref, mine_ref, other_ref, weight_ref, *refs):
        outs, (total, *rounded, near_held, far_held, buffer, arrived, gone, here) = refs[:turns], refs[turns:]
        brought = [
            pltpu.make_async_copy(mine_ref, near_held, here.at[0]),
            pltpu.make_async_copy(other_ref, far_held, here.at[1]),
        ]
        for copy in brought:
            copy.start()

        def leave(turn):
            return pltpu.make_async_copy(rounded[turn], outs[turn], gone.at[turn])


        def place(step):
            block = lax.rem(lax.rem(step, steps) + meta_ref[5] * near, steps)
            dest = meta_ref[6 + first_slot + step // steps]
            return (
                pl.ds(pl.multiple_of(block * DEPTH, DEPTH), DEPTH),
                pl.ds(pl.multiple_of(dest * columns, columns), columns),
            )

        def multiply(step, block):
            inner = lax.rem(step, steps)
            spot = pl.ds(pl.multiple_of(lax.rem(inner, near) * DEPTH, DEPTH), DEPTH)

            @pl.when(step == 0)
            def _():
                for copy in brought:
                    copy.wait()

            @pl.when(inner == 0)
            def _():
                total[...] = jnp.dot(near_held[:, spot], block, preferred_element_type=jnp.float32)

            @pl.when((inner > 0) & (inner < near))
            def _():
                total[...] += jnp.dot(near_held[:, spot], block, preferred_element_type=jnp.float32)

            @pl.when(inner >= near)
            def _():
                total[...] += jnp.dot(far_held[:, spot], block, preferred_element_type=jnp.float32)

            for turn in range(turns):
                @pl.when(step == turn * steps + steps - 1)
                def _():
                    rounded[turn][...] = total[...].astype(rounded[turn].dtype)
                    leave(turn).start()

        streamed(weight_ref, place, turns * steps, buffer, arrived, multiply)
        for turn in range(turns):
            leave(turn).wait()

    return order.call(
        body,
        [jax.ShapeDtypeStruct((rows, columns), kind) for kind in kinds],
        [
            pltpu.VMEM((rows, columns), jnp.float32),
            *[pltpu.VMEM((rows, columns), kind) for kind in kinds],
            pltpu.VMEM((rows, width), jnp.bfloat16),
            pltpu.VMEM((rows, width), jnp.bfloat16),
            pltpu.VMEM((BUFFERS, DEPTH, columns), jnp.bfloat16),
            pltpu.SemaphoreType.DMA((BUFFERS,)),
            pltpu.SemaphoreType.DMA((turns,)),
            pltpu.SemaphoreType.DMA((2,)),
        ],
        [meta, mine, other, weight],
        [pltpu.SMEM, pl.ANY, pl.ANY, pl.ANY],
        "output_parts",
        [pl.ANY] * turns,
        cost=2 * turns * weight.shape[0] * columns,
    )


def line_shards(activations, norm_gain, query_weight, kv_weight, out_weight, block_ids, clean_mask):
    col, row, seq = (lax.axis_index(axis) for axis in ("col", "row", "seq"))
    slab, width = activations.shape
    bounds = chunk_bounds(slab)
    half = slab // 2
    swap = ((0, 1), (1, 0))
    at_end = (col == 0) | (col == LINE - 1)
    meta = jnp.concatenate(
        [
            jnp.asarray(FEATURE_ORDER, jnp.int32)[col],
            jnp.stack([at_end.astype(jnp.int32), row.astype(jnp.int32)]),
            jnp.asarray(DEST_ORDER, jnp.int32)[col],
            col[None],
        ]
    )

    def send_far(beside, across):
        return hop(beside, MIDDLE), hop(across, OUTER_OUT)

    ids = block_ids[None, :]
    cut = jnp.where(clean_mask == 1, block_ids, jnp.iinfo(jnp.int32).max)[None, :]
    my_ids = lax.dynamic_slice_in_dim(block_ids, seq * slab, slab, 0)
    my_ids = jnp.broadcast_to(my_ids[:, None], (slab, HD))

    inverse = jnp.exp(jnp.arange(HD // 2, dtype=jnp.float32) * (-2.0 * math.log(rope_base) / HD))
    positions = seq * slab + jnp.arange(slab, dtype=jnp.int32)
    angles = positions.astype(jnp.float32)[:, None] * inverse[None, :]
    rope_cosine = jnp.concatenate([jnp.cos(angles)] * 2, axis=1)
    rope_sine = jnp.concatenate([-jnp.sin(angles), jnp.sin(angles)], axis=1)

    order = Order()
    gain = norm_gain[None, :]
    first_rows = gain_rows(order, activations, gain, bounds[0][1])
    beside, across = hop(first_rows, OUTER_IN + OUTER_OUT), hop(first_rows, MIDDLE)

    around = [[(i, (i + offset) % LINE) for i in range(LINE)] for offset in range(1, LINE)]
    kept, given, gained = key_value_terms(order, meta, activations, gain, kv_weight, bounds[1:])
    gained = [first_rows] + gained
    given = hop(given, swap, "row")
    beside, across, my_ids, cut, rope_cosine, rope_sine = order.arrive(
        beside, across, my_ids, cut, rope_cosine, rope_sine
    )
    far = send_far(beside, across)
    own, *shares = key_value_shares(order, meta, kept, given)
    shares = [own] + [hop(share, pairs) for share, pairs in zip(shares, around)]
    pairs, cosine, sine = key_value_rows(order, meta, shares, rope_cosine, rope_sine)
    pairs = lax.all_gather(pairs, ("seq", "row"), axis=0, tiled=True)
    far_middle, far_end = order.arrive(*far)
    farthest = hop(far_middle, OUTER_OUT)

    out, waiting = None, None
    for i in range(len(bounds)):
        more = i + 1 < len(bounds)
        (so_far,) = project(
            order,
            meta,
            ((0, (0,)), (1, (1,)), (2, (2, 3))),
            (gained[i], beside, across, far_end),
            None,
            query_weight,
            False,
        )
        if more:
            farthest, gained[i + 1] = order.arrive(farthest, gained[i + 1])
            beside, across = hop(gained[i + 1], OUTER_IN + OUTER_OUT), hop(gained[i + 1], MIDDLE)
        mine, other = project(order, meta, ((3, (0, 1)),), (far_middle, farthest), so_far, query_weight, True)
        other = hop(other, swap, "row")
        if waiting is not None:
            fourth, outer, middle = last_sums(order, meta, *waiting)
            waiting = (fourth, hop(outer, OUTER_IN + OUTER_OUT), hop(middle, MIDDLE))
        attended = attend(order, mine, other, bounds[i], cosine, sine, pairs, my_ids, ids, cut)
        other_attended = hop(attended, swap, "row")
        if more:
            beside, across = order.arrive(beside, across)
            far_middle, far_end = send_far(beside, across)
        first, second = output_parts(
            order, meta, 0, attended, other_attended, out_weight, (jnp.bfloat16, jnp.bfloat16)
        )
        inward, inward_next = hop(first, OUTER_IN), hop(second, OUTER_IN)
        third, fourth = output_parts(
            order, meta, 2, attended, other_attended, out_weight, (jnp.bfloat16, jnp.float32)
        )
        if waiting is not None:
            out = final_rows(order, out, slab, bounds[i - 1], waiting)
        if more:
            far_middle, far_end = order.arrive(far_middle, far_end)
            farthest = hop(far_middle, OUTER_OUT)
        (middle,) = order.add([(second, inward)], [jnp.bfloat16])
        waiting = (first, third, fourth, hop(middle, MIDDLE), inward_next)
    fourth, outer, middle = last_sums(order, meta, *waiting)
    outer, middle = hop(outer, OUTER_IN + OUTER_OUT), hop(middle, MIDDLE)
    return final_rows(order, out, slab, bounds[-1], (fourth, outer, middle))


def solution(mesh):
    placed = (
        P("seq", ("row", "col")),
        P(("row", "col")),
        P("row", "col"),
        P("row", None, None),
        P("col", "row"),
        P(),
        P(),
    )
    on_line = mesh.shape["col"] == LINE == KVH and mesh.shape["row"] == 2
    return jax.shard_map(
        line_shards if on_line else gathered_shards,
        mesh=mesh,
        in_specs=placed,
        out_specs=P("seq", ("row", "col")),
        check_vma=False,
    )
```

```python
import functools
import math

import jax
import jax.numpy as jnp
from jax import lax
from jax.experimental import pallas as pl
from jax.experimental.pallas import tpu as pltpu
from jax.sharding import PartitionSpec as P

D = 16384
HD = 128
QH = 64
KVH = 4


rope_base = 500000.0
norm_eps = 1e-05


def rotate(values, positions):
    half_dim = values.shape[-1] // 2
    inverse = jnp.exp(
        jnp.arange(half_dim, dtype=jnp.float32) * (-2.0 * math.log(rope_base) / values.shape[-1])
    )
    angles = positions.astype(jnp.float32)[:, None] * inverse[None, :]
    cosine = jnp.cos(angles)
    sine_part = jnp.sin(angles)
    first_half = values[..., :half_dim]
    second_half = values[..., half_dim:]
    return jnp.concatenate(
        [
            first_half * cosine - second_half * sine_part,
            second_half * cosine + first_half * sine_part,
        ],
        axis=-1,
    )


def gathered_shards(activations, norm_gain, query_weight, kv_weight, out_weight, block_ids, clean_mask):
    row_count = lax.axis_size("row")
    col_index = lax.axis_index("col")
    seq_index = lax.axis_index("seq")
    slab_len = activations.shape[0]
    col_heads = query_weight.shape[1] // HD
    dev_heads = col_heads // row_count
    group_size = QH // KVH
    wide_input = activations.astype(jnp.float32)
    squares = lax.psum(jnp.sum(wide_input * wide_input, axis=1), ("row", "col"))
    scaling = lax.rsqrt(squares / D + norm_eps)
    normed = (wide_input * scaling[:, None] * norm_gain[None, :]).astype(jnp.bfloat16)
    panel_rows = lax.all_gather(normed, "col", axis=1, tiled=True)
    kv_count = max(col_heads // group_size, 1)
    kv_first = col_index * col_heads // group_size
    kv_tiles = lax.dynamic_slice_in_dim(kv_weight, kv_first * HD, kv_count * HD, 2)
    kv_term = jnp.einsum("td,dke->kte", panel_rows, kv_tiles, preferred_element_type=jnp.float32)
    columns = query_weight
    columns = columns.reshape(columns.shape[0], dev_heads * lax.axis_size("row"), HD)
    query_sum = lax.psum_scatter(
        jnp.einsum("td,dhe->hte", panel_rows, columns, preferred_element_type=jnp.float32),
        "row",
        scatter_dimension=0,
        tiled=True,
    )
    kv_sum = lax.psum(kv_term, "row")
    key_raw = kv_sum[0]
    value_rows = kv_sum[1].astype(jnp.bfloat16)
    positions = seq_index * slab_len + jnp.arange(slab_len, dtype=jnp.int32)
    key_rows = rotate(key_raw, positions).astype(jnp.bfloat16)
    queries = rotate(query_sum, positions).astype(jnp.bfloat16)
    my_blocks = lax.dynamic_slice_in_dim(block_ids, seq_index * slab_len, slab_len, 0)
    score_scale = 1.0 / math.sqrt(HD)
    key_piece = lax.all_gather(key_rows, "seq", axis=0, tiled=True)
    value_piece = lax.all_gather(value_rows, "seq", axis=0, tiled=True)
    visible = (block_ids[None, :] == my_blocks[:, None]) | (
        block_ids[None, :] < my_blocks[:, None]
    ) & (clean_mask[None, :] == 1)
    scores = (
        jnp.einsum("hte,ne->htn", queries, key_piece, preferred_element_type=jnp.float32)
        * score_scale
    )
    weights = jnp.where(visible[None, :, :], jnp.exp(scores), jnp.zeros_like(scores))
    numerator = jnp.einsum(
        "htn,ne->hte", weights.astype(jnp.bfloat16), value_piece, preferred_element_type=jnp.float32
    )
    denominator = jnp.sum(weights, axis=2)
    numerator, denominator = (numerator, denominator)
    attended = (numerator / denominator[:, :, None]).astype(jnp.bfloat16)
    out_cols = out_weight.shape[1]
    portion = lax.all_gather(attended, "row", axis=0, tiled=True)
    heads_here = portion.shape[0]
    out_rows = out_weight
    out_rows = out_rows.reshape(heads_here, HD, out_cols)
    partial_out = jnp.einsum("hte,hed->td", portion, out_rows, preferred_element_type=jnp.float32)
    projected = lax.psum_scatter(partial_out, "col", scatter_dimension=1, tiled=True)
    return projected.astype(jnp.bfloat16)


LINE = 4
OUTER_IN = ((0, 1), (3, 2))
OUTER_OUT = ((2, 3), (1, 0))
MIDDLE = ((1, 2), (2, 1))
DEST_ORDER = ((3, 2, 1, 0), (0, 3, 2, 1), (3, 0, 1, 2), (0, 1, 2, 3))
FEATURE_ORDER = ((0, 1, 2, 3), (1, 0, 2, 3), (2, 3, 1, 0), (3, 2, 1, 0))
CHUNK_SHARES = (12, 12, 8)
DEPTH = 512
BUFFERS = 4
COST_SCALE = 1.0
EXTRA = 16


def hop(values, pairs, axis="col"):
    return lax.ppermute(values, axis, list(pairs))


def chunk_bounds(slab):
    whole = sum(CHUNK_SHARES)
    marks = [slab * sum(CHUNK_SHARES[:i]) // whole // 16 * 16 for i in range(len(CHUNK_SHARES))] + [slab]
    return list(zip(marks[:-1], marks[1:]))


class Order:
    def __init__(self):
        self.token = []

    def call(self, body, outs, scratch, inputs, spaces, name, out_spaces=None, aliases=None, cost=1_000_000):
        count, given = len(inputs), len(outs)
        tokens = list(self.token)

        def kernel(*refs):
            refs = refs[:count] + refs[count + len(tokens) :]
            body(*refs[: count + given], *refs[count + given + 1 :])

        results = pl.pallas_call(
            kernel,
            out_shape=list(outs) + [jax.ShapeDtypeStruct((8, HD), jnp.float32)],
            in_specs=[pl.BlockSpec(memory_space=space) for space in spaces]
            + [pl.BlockSpec(memory_space=pl.ANY)] * len(tokens),
            out_specs=[pl.BlockSpec(memory_space=space) for space in (out_spaces or [pltpu.VMEM] * given)]
            + [pl.BlockSpec(memory_space=pl.ANY)],
            scratch_shapes=scratch,
            input_output_aliases=aliases or {},
            compiler_params=pltpu.CompilerParams(vmem_limit_bytes=36 << 20),
            cost_estimate=pl.CostEstimate(flops=0, bytes_accessed=int(cost * COST_SCALE), transcendentals=0),
            name=name,
        )(*inputs, *tokens)
        self.token = [results[-1]]
        return results[:-1]

    def arrive(self, *arrays):
        def body(*refs):
            pass

        outs = [jax.ShapeDtypeStruct(array.shape, array.dtype) for array in arrays]
        spaces = [pl.ANY] * len(arrays)
        return self.call(body, outs, [], arrays, spaces, "arrive", spaces, {i: i for i in range(len(arrays))}, 0)

    def add(self, groups, kinds):
        flat = [array for group in groups for array in group]

        def body(*refs):
            ins, outs = refs[: len(flat)], refs[len(flat) :]
            for group, out in zip(groups, outs):
                part, ins = ins[: len(group)], ins[len(group) :]
                out[...] = sum(ref[...].astype(jnp.float32) for ref in part).astype(out.dtype)

        outs = [jax.ShapeDtypeStruct(group[0].shape, kind) for group, kind in zip(groups, kinds)]
        return self.call(body, outs, [], flat, [pltpu.VMEM] * len(flat), "adding")


def last_sums(order, meta, first, third, fourth, through, inward_next):
    def body(meta_ref, first_ref, third_ref, through_ref, next_ref, outer, middle):
        @pl.when(meta_ref[4] == 1)
        def _():
            outer[...] = third_ref[...]

        @pl.when(meta_ref[4] == 0)
        def _():
            wide = first_ref[...].astype(jnp.float32) + through_ref[...].astype(jnp.float32)
            outer[...] = wide.astype(outer.dtype)

        wide = third_ref[...].astype(jnp.float32) + next_ref[...].astype(jnp.float32)
        middle[...] = wide.astype(middle.dtype)

    outer, middle = order.call(
        body,
        [jax.ShapeDtypeStruct(first.shape, first.dtype)] * 2,
        [],
        [meta, first, third, through, inward_next],
        [pltpu.SMEM] + [pltpu.VMEM] * 4,
        "last_sums",
    )
    return fourth, outer, middle


def gain_rows(order, activations, gain, rows):
    width = activations.shape[1]

    def body(source, gain_ref, out, held, here):
        copy = pltpu.make_async_copy(source.at[:rows, :], held, here)
        copy.start()
        copy.wait()
        out[...] = (held[...].astype(jnp.float32) * gain_ref[...]).astype(out.dtype)

    return order.call(
        body,
        [jax.ShapeDtypeStruct((rows, width), jnp.bfloat16)],
        [pltpu.VMEM((rows, width), jnp.bfloat16), pltpu.SemaphoreType.DMA(())],
        [activations, gain],
        [pl.ANY, pltpu.VMEM],
        "gain_rows",
    )[0]


def key_value_terms(order, meta, activations, gain, weight, bounds):
    slab, width = activations.shape
    columns = weight.shape[1] * weight.shape[2]
    half = slab // 2
    steps = width // DEPTH

    def body(meta_ref, source, gain_ref, weight_ref, kept, given, *refs):
        outs, (gained, total, held, buffer, here, arrived) = refs[:-6], refs[-6:]
        brought = pltpu.make_async_copy(source, held, here)
        brought.start()

        def place(step):
            return pl.ds(meta_ref[10] * width + step * DEPTH, DEPTH)

        def multiply(step, block):
            @pl.when(step == 0)
            def _():
                brought.wait()
                wide = held[...].astype(jnp.float32)
                gained[...] = (wide * gain_ref[...]).astype(gained.dtype)
                total[...] = jnp.zeros_like(total)

            left = gained[:, pl.ds(pl.multiple_of(step * DEPTH, DEPTH), DEPTH)]
            total[...] += jnp.dot(left, block.reshape(DEPTH, columns), preferred_element_type=jnp.float32)

        streamed(weight_ref, place, steps, buffer, arrived, multiply)
        wide = held[...].astype(jnp.float32)
        squares = jnp.sum(wide * wide, axis=1, keepdims=True)
        diagonal = lax.broadcasted_iota(jnp.int32, (HD, HD), 0) == lax.broadcasted_iota(jnp.int32, (HD, HD), 1)
        for out, which in ((given, 1 - meta_ref[5]), (kept, meta_ref[5])):
            out[:half, :] = total[pl.ds(pl.multiple_of(which * half, half), half), :]
            out[half:, :] = jnp.zeros((EXTRA, columns), jnp.float32)
            for block in range(slab // HD):
                part = jnp.broadcast_to(squares[block * HD : (block + 1) * HD], (HD, HD))
                out[half : half + 1, block * HD : (block + 1) * HD] = jnp.sum(
                    jnp.where(diagonal, part, 0.0), axis=0, keepdims=True
                )
        for (low, high), out in zip(bounds, outs):
            out[...] = gained[low:high, :]

    kept, given, *gained = order.call(
        body,
        [jax.ShapeDtypeStruct((half + EXTRA, columns), jnp.float32)] * 2
        + [jax.ShapeDtypeStruct((high - low, width), jnp.bfloat16) for low, high in bounds],
        [
            pltpu.VMEM((slab, width), jnp.bfloat16),
            pltpu.VMEM((slab, columns), jnp.float32),
            pltpu.VMEM((slab, width), jnp.bfloat16),
            pltpu.VMEM((BUFFERS, DEPTH) + weight.shape[1:], jnp.bfloat16),
            pltpu.SemaphoreType.DMA(()),
            pltpu.SemaphoreType.DMA((BUFFERS,)),
        ],
        [meta, activations, gain, weight],
        [pltpu.SMEM, pl.ANY, pltpu.VMEM, pl.ANY],
        "key_value_terms",
        cost=15_000_000,
    )
    return kept, given, gained


def key_value_shares(order, meta, kept, arrived):
    rows, columns = kept.shape[0] - EXTRA, kept.shape[1]
    heads = columns // (2 * HD)

    def body(meta_ref, kept_ref, arrived_ref, *outs):
        squares = kept_ref[rows : rows + 1, :] + arrived_ref[rows : rows + 1, :]
        pieces, rest = [], squares
        for _ in range(3):
            piece = rest.astype(jnp.bfloat16)
            pieces.append(piece.astype(jnp.float32))
            rest = rest - pieces[-1]
        blocks = 2 * rows // HD
        lines = [
            jnp.concatenate([piece[:, i * HD : (i + 1) * HD] for piece in (pieces[0], pieces[1])], axis=1)
            for i in range(blocks)
        ] + [
            jnp.concatenate([pieces[2][:, i * HD : (i + 1) * HD]] * 2, axis=1) for i in range(blocks)
        ]
        lines = jnp.concatenate(lines + [jnp.zeros((EXTRA - 2 * blocks, 2 * HD), jnp.float32)], axis=0)
        for offset, out in enumerate(outs):
            head = lax.rem(meta_ref[10] + offset, heads)
            for part in range(2):
                spot = pl.ds(pl.multiple_of(part * heads * HD + head * HD, HD), HD)
                both = kept_ref[:rows, spot] + arrived_ref[:rows, spot]
                out[:rows, part * HD : (part + 1) * HD] = both.astype(out.dtype)
            out[rows:, :] = lines.astype(out.dtype)

    return order.call(
        body,
        [jax.ShapeDtypeStruct((rows + EXTRA, 2 * HD), jnp.float32)]
        + [jax.ShapeDtypeStruct((rows + EXTRA, 2 * HD), jnp.bfloat16)] * (heads - 1),
        [],
        [meta, kept, arrived],
        [pltpu.SMEM, pltpu.VMEM, pltpu.VMEM],
        "key_value_shares",
    )


def key_value_rows(order, meta, shares, cosine, sine):
    rows = shares[0].shape[0] - EXTRA
    blocks = 2 * rows // HD

    def body(meta_ref, *refs):
        share_refs, (cosine_ref, sine_ref, out, cosine_out, sine_out, scaling) = refs[: len(shares)], refs[len(shares) :]
        total = sum(ref[...].astype(jnp.float32) for ref in share_refs)
        diagonal = lax.broadcasted_iota(jnp.int32, (HD, HD), 0) == lax.broadcasted_iota(jnp.int32, (HD, HD), 1)
        for block in range(blocks):
            line = total[rows + block : rows + block + 1, :]
            last = total[rows + blocks + block : rows + blocks + block + 1, :HD]
            squares = line[:, :HD] + line[:, HD:] + last
            factor = lax.rsqrt(squares / D + norm_eps)
            column = jnp.sum(jnp.where(diagonal, factor, 0.0), axis=1, keepdims=True)
            scaling[block * HD : (block + 1) * HD, :] = jnp.broadcast_to(column, (HD, HD))
        cosine_out[...] = cosine_ref[...] * scaling[...]
        sine_out[...] = sine_ref[...] * scaling[...]
        spot = pl.ds(pl.multiple_of(meta_ref[5] * rows, rows), rows)
        raw = total[:rows, :HD]
        turned = pltpu.roll(raw, HD // 2, 1)
        out[:, :HD] = (raw * cosine_out[spot, :] + turned * sine_out[spot, :]).astype(out.dtype)
        out[:, HD:] = (total[:rows, HD:] * scaling[spot, :]).astype(out.dtype)

    inputs = [meta, *shares, cosine, sine]
    return order.call(
        body,
        [jax.ShapeDtypeStruct((rows, 2 * HD), jnp.bfloat16)] + [jax.ShapeDtypeStruct(cosine.shape, jnp.float32)] * 2,
        [pltpu.VMEM(cosine.shape, jnp.float32)],
        inputs,
        [pltpu.SMEM] + [pltpu.VMEM] * (len(inputs) - 1),
        "key_value_rows",
    )


def final_rows(order, so_far, slab, bounds, parts):
    rows, width = parts[0].shape

    def body(*refs):
        ins = refs[: len(parts)]
        out, held, here = refs[-3:]
        held[...] = sum(ref[...].astype(jnp.float32) for ref in ins).astype(held.dtype)
        copy = pltpu.make_async_copy(held, out.at[slice(*bounds), :], here)
        copy.start()
        copy.wait()

    inputs = list(parts) + ([] if so_far is None else [so_far])
    return order.call(
        body,
        [jax.ShapeDtypeStruct((slab, width), jnp.bfloat16)],
        [pltpu.VMEM((rows, width), jnp.bfloat16), pltpu.SemaphoreType.DMA(())],
        inputs,
        [pltpu.VMEM] * len(parts) + [pl.ANY] * (len(inputs) - len(parts)),
        "final_rows",
        [pl.ANY],
        {} if so_far is None else {len(parts): 0},
    )[0]


def streamed(weight_ref, place, steps, buffer, arrived, multiply):
    depth = buffer.shape[0]

    def copy(step):
        spot = lax.rem(step, depth)
        return pltpu.make_async_copy(weight_ref.at[place(step)], buffer.at[spot], arrived.at[spot])

    for step in range(min(depth, steps)):
        copy(jnp.int32(step)).start()

    def one(step, carry):
        copy(step).wait()
        multiply(step, buffer[lax.rem(step, depth)])

        @pl.when(step + depth < steps)
        def _():
            copy(step + depth).start()

        return carry

    lax.fori_loop(0, steps, one, 0)


def project(order, meta, slots, features, so_far, weight, split):
    rows, width = features[0].shape
    columns = weight.shape[1]
    steps = columns // DEPTH
    first, turns = slots[0][0], len(slots)

    def body(meta_ref, weight_ref, *refs):
        if so_far is not None:
            so_far_ref, refs = refs[0], refs[1:]
        feature_refs, refs = refs[: len(features)], refs[len(features) :]
        if split:
            outs, (total, held, buffer, here, arrived) = refs[:-5], refs[-5:]
        else:
            (total,), (held, buffer, here, arrived) = refs[:-4], refs[-4:]
        if so_far is not None:
            brought = pltpu.make_async_copy(so_far_ref, total, here.at[turns])
            brought.start()
        for turn, (_, choices) in enumerate(slots):
            def start(which):
                pltpu.make_async_copy(feature_refs[which], held.at[turn], here.at[turn]).start()

            if len(choices) == 1:
                start(choices[0])
            else:
                pl.when(meta_ref[4] == 0)(functools.partial(start, choices[0]))
                pl.when(meta_ref[4] == 1)(functools.partial(start, choices[1]))
        def place(step):
            rows_of = meta_ref[first + step // steps]
            return (
                pl.ds(pl.multiple_of(rows_of * width, width), width),
                pl.ds(pl.multiple_of(lax.rem(step, steps) * DEPTH, DEPTH), DEPTH),
            )

        def multiply(step, block):
            turn, inner = step // steps, lax.rem(step, steps)
            spot = pl.ds(pl.multiple_of(inner * DEPTH, DEPTH), DEPTH)

            if so_far is not None:
                pl.when(step == 0)(brought.wait)

            @pl.when(inner == 0)
            def _():
                pltpu.make_async_copy(feature_refs[0], held.at[turn], here.at[turn]).wait()

            part = jnp.dot(held[turn], block, preferred_element_type=jnp.float32)
            if so_far is not None:
                total[:, spot] += part
            else:
                @pl.when(turn == 0)
                def _():
                    total[:, spot] = part

                @pl.when(turn > 0)
                def _():
                    total[:, spot] += part

        streamed(weight_ref, place, turns * steps, buffer, arrived, multiply)
        if split:
            half = columns // 2
            mine = meta_ref[5]
            outs[0][...] = total[:, pl.ds(pl.multiple_of(mine * half, half), half)]
            outs[1][...] = total[:, pl.ds(pl.multiple_of((1 - mine) * half, half), half)]

    whole = jax.ShapeDtypeStruct((rows, columns), jnp.float32)
    halves = jax.ShapeDtypeStruct((rows, columns // 2), jnp.float32)
    inputs = [meta, weight] + ([] if so_far is None else [so_far]) + list(features)
    spaces = [pltpu.SMEM, pl.ANY] + ([] if so_far is None else [pl.ANY]) + [pl.ANY] * len(features)
    return order.call(
        body,
        [halves, halves] if split else [whole],
        ([pltpu.VMEM((rows, columns), jnp.float32)] if split else [])
        + [
            pltpu.VMEM((turns, rows, width), jnp.bfloat16),
            pltpu.VMEM((BUFFERS, width, DEPTH), jnp.bfloat16),
            pltpu.SemaphoreType.DMA((turns + 1,)),
            pltpu.SemaphoreType.DMA((BUFFERS,)),
        ],
        inputs,
        spaces,
        "project",
        cost=2 * turns * width * columns,
    )


def attend(order, mine, arrived, bounds, cosine, sine, pairs, own_ids, ids, cut):
    rows, width = mine.shape
    key_count = pairs.shape[0]
    tile = min(512, key_count)
    spot_rows = slice(*bounds)
    factor = math.log2(math.e) / math.sqrt(HD)

    def body(
        mine_ref, arrived_ref, cosine_ref, sine_ref, pair_ref, own_ids_ref, ids_ref, cut_ref, out_ref, bias, values
    ):
        values[:, :HD] = pair_ref[:, HD:]
        values[:, HD:] = jnp.ones((key_count, HD), values.dtype)
        own = own_ids_ref[spot_rows, :1]
        for first in range(0, key_count, tile):
            spot = slice(first, first + tile)
            seen = (ids_ref[:, spot] == own) | (cut_ref[:, spot] < own)
            bias[:, spot] = jnp.where(seen, 0.0, -jnp.inf)

        def one_head(head, carry):
            place = pl.ds(pl.multiple_of(head * HD, HD), HD)
            raw = mine_ref[:, place] + arrived_ref[:, place]
            turned = pltpu.roll(raw, HD // 2, 1)
            query = (raw * cosine_ref[spot_rows, :] + turned * sine_ref[spot_rows, :]).astype(jnp.bfloat16)
            summed = jnp.zeros((rows, values.shape[1]), jnp.float32)
            for first in range(0, key_count, tile):
                spot = slice(first, first + tile)
                scores = lax.dot_general(
                    query, pair_ref[spot, :HD], (((1,), (1,)), ((), ())), preferred_element_type=jnp.float32
                )
                weights = jnp.exp2(scores * factor + bias[:, spot])
                summed += jnp.dot(weights.astype(jnp.bfloat16), values[spot, :], preferred_element_type=jnp.float32)
            out_ref[:, place] = (summed[:, :HD] / summed[:, HD:]).astype(jnp.bfloat16)
            return carry

        lax.fori_loop(0, width // HD, one_head, 0, unroll=2)

    return order.call(
        body,
        [jax.ShapeDtypeStruct((rows, width), jnp.bfloat16)],
        [pltpu.VMEM((rows, key_count), jnp.float32), pltpu.VMEM((key_count, 2 * HD), jnp.bfloat16)],
        [mine, arrived, cosine, sine, pairs, own_ids, ids, cut],
        [pltpu.VMEM] * 8,
        "attend",
        cost=20_000_000,
    )[0]


def output_parts(order, meta, first_slot, mine, other, weight, kinds):
    rows, width = mine.shape
    depth = weight.shape[0]
    columns = weight.shape[1] // LINE
    steps = columns // DEPTH
    turns = len(kinds)

    def body(meta_ref, mine_ref, other_ref, weight_ref, *refs):
        outs, (*rounded, held, buffer, arrived, gone, here) = refs[:turns], refs[turns:]
        core = meta_ref[5]
        brought = [
            pltpu.make_async_copy(source, held.at[:, pl.ds(pl.multiple_of(which * width, width), width)], here.at[i])
            for i, (source, which) in enumerate(((mine_ref, core), (other_ref, 1 - core)))
        ]
        for copy in brought:
            copy.start()

        def leave(turn):
            return pltpu.make_async_copy(rounded[turn], outs[turn], gone.at[turn])

        def place(step):
            dest = meta_ref[6 + first_slot + step // steps]
            spot = dest * columns + lax.rem(step, steps) * DEPTH
            return (slice(None), pl.ds(pl.multiple_of(spot, DEPTH), DEPTH))

        def multiply(step, block):
            inner = lax.rem(step, steps)

            @pl.when(step == 0)
            def _():
                for copy in brought:
                    copy.wait()

            part = jnp.dot(held[...], block, preferred_element_type=jnp.float32)
            for turn in range(turns):
                @pl.when(step // steps == turn)
                def _():
                    spot = pl.ds(pl.multiple_of(inner * DEPTH, DEPTH), DEPTH)
                    rounded[turn][:, spot] = part.astype(rounded[turn].dtype)
                    pl.when(inner == steps - 1)(leave(turn).start)

        streamed(weight_ref, place, turns * steps, buffer, arrived, multiply)
        for turn in range(turns):
            leave(turn).wait()

    return order.call(
        body,
        [jax.ShapeDtypeStruct((rows, columns), kind) for kind in kinds],
        [
            *[pltpu.VMEM((rows, columns), kind) for kind in kinds],
            pltpu.VMEM((rows, depth), jnp.bfloat16),
            pltpu.VMEM((BUFFERS, depth, DEPTH), jnp.bfloat16),
            pltpu.SemaphoreType.DMA((BUFFERS,)),
            pltpu.SemaphoreType.DMA((turns,)),
            pltpu.SemaphoreType.DMA((2,)),
        ],
        [meta, mine, other, weight],
        [pltpu.SMEM, pl.ANY, pl.ANY, pl.ANY],
        "output_parts",
        [pl.ANY] * turns,
        cost=2 * turns * depth * columns,
    )


def line_shards(activations, norm_gain, query_weight, kv_weight, out_weight, block_ids, clean_mask):
    col, row, seq = (lax.axis_index(axis) for axis in ("col", "row", "seq"))
    slab, width = activations.shape
    bounds = chunk_bounds(slab)
    half = slab // 2
    swap = ((0, 1), (1, 0))
    at_end = (col == 0) | (col == LINE - 1)
    meta = jnp.concatenate(
        [
            jnp.asarray(FEATURE_ORDER, jnp.int32)[col],
            jnp.stack([at_end.astype(jnp.int32), row.astype(jnp.int32)]),
            jnp.asarray(DEST_ORDER, jnp.int32)[col],
            col[None],
        ]
    )

    def send_far(beside, across):
        return hop(beside, MIDDLE), hop(across, OUTER_OUT)

    ids = block_ids[None, :]
    cut = jnp.where(clean_mask == 1, block_ids, jnp.iinfo(jnp.int32).max)[None, :]
    my_ids = lax.dynamic_slice_in_dim(block_ids, seq * slab, slab, 0)
    my_ids = jnp.broadcast_to(my_ids[:, None], (slab, HD))

    inverse = jnp.exp(jnp.arange(HD // 2, dtype=jnp.float32) * (-2.0 * math.log(rope_base) / HD))
    positions = seq * slab + jnp.arange(slab, dtype=jnp.int32)
    angles = positions.astype(jnp.float32)[:, None] * inverse[None, :]
    rope_cosine = jnp.concatenate([jnp.cos(angles)] * 2, axis=1)
    rope_sine = jnp.concatenate([-jnp.sin(angles), jnp.sin(angles)], axis=1)

    order = Order()
    gain = norm_gain[None, :]
    first_rows = gain_rows(order, activations, gain, bounds[0][1])
    beside, across = hop(first_rows, OUTER_IN + OUTER_OUT), hop(first_rows, MIDDLE)

    around = [[(i, (i + offset) % LINE) for i in range(LINE)] for offset in range(1, LINE)]
    kept, given, gained = key_value_terms(order, meta, activations, gain, kv_weight, bounds[1:])
    gained = [first_rows] + gained
    given = hop(given, swap, "row")
    beside, across, my_ids, cut, rope_cosine, rope_sine = order.arrive(
        beside, across, my_ids, cut, rope_cosine, rope_sine
    )
    far = send_far(beside, across)
    own, *shares = key_value_shares(order, meta, kept, given)
    shares = [own] + [hop(share, pairs) for share, pairs in zip(shares, around)]
    pairs, cosine, sine = key_value_rows(order, meta, shares, rope_cosine, rope_sine)
    pairs = lax.all_gather(pairs, ("seq", "row"), axis=0, tiled=True)
    far_middle, far_end = order.arrive(*far)
    farthest = hop(far_middle, OUTER_OUT)

    out, waiting = None, None
    for i in range(len(bounds)):
        more = i + 1 < len(bounds)
        (so_far,) = project(
            order,
            meta,
            ((0, (0,)), (1, (1,)), (2, (2, 3))),
            (gained[i], beside, across, far_end),
            None,
            query_weight,
            False,
        )
        if more:
            farthest, gained[i + 1] = order.arrive(farthest, gained[i + 1])
            beside, across = hop(gained[i + 1], OUTER_IN + OUTER_OUT), hop(gained[i + 1], MIDDLE)
        mine, other = project(order, meta, ((3, (0, 1)),), (far_middle, farthest), so_far, query_weight, True)
        other = hop(other, swap, "row")
        if waiting is not None:
            fourth, outer, middle = last_sums(order, meta, *waiting)
            waiting = (fourth, hop(outer, OUTER_IN + OUTER_OUT), hop(middle, MIDDLE))
        attended = attend(order, mine, other, bounds[i], cosine, sine, pairs, my_ids, ids, cut)
        other_attended = hop(attended, swap, "row")
        spread_out = lambda slot, *kinds: output_parts(
            order, meta, slot, attended, other_attended, out_weight, kinds
        )
        if more:
            first, second = spread_out(0, jnp.bfloat16, jnp.bfloat16)
            inward, inward_next = hop(first, OUTER_IN), hop(second, OUTER_IN)
            beside, across = order.arrive(beside, across)
            far_middle, far_end = send_far(beside, across)
            third, fourth = spread_out(2, jnp.bfloat16, jnp.float32)
        else:
            (first,) = spread_out(0, jnp.bfloat16)
            inward = hop(first, OUTER_IN)
            second, third, fourth = spread_out(1, jnp.bfloat16, jnp.bfloat16, jnp.float32)
            inward_next = hop(second, OUTER_IN)
        if waiting is not None:
            out = final_rows(order, out, slab, bounds[i - 1], waiting)
        if more:
            far_middle, far_end = order.arrive(far_middle, far_end)
            farthest = hop(far_middle, OUTER_OUT)
        (middle,) = order.add([(second, inward)], [jnp.bfloat16])
        waiting = (first, third, fourth, hop(middle, MIDDLE), inward_next)
    fourth, outer, middle = last_sums(order, meta, *waiting)
    outer, middle = hop(outer, OUTER_IN + OUTER_OUT), hop(middle, MIDDLE)
    return final_rows(order, out, slab, bounds[-1], (fourth, outer, middle))


def solution(mesh):
    placed = (
        P("seq", ("row", "col")),
        P(("row", "col")),
        P("row", "col"),
        P("row", None, None),
        P("col", "row"),
        P(),
        P(),
    )
    on_line = mesh.shape["col"] == LINE == KVH and mesh.shape["row"] == 2
    return jax.shard_map(
        line_shards if on_line else gathered_shards,
        mesh=mesh,
        in_specs=placed,
        out_specs=P("seq", ("row", "col")),
        check_vma=False,
    )
```

```python
import functools
import math

import jax
import jax.numpy as jnp
from jax import lax
from jax.experimental import pallas as pl
from jax.experimental.pallas import tpu as pltpu
from jax.sharding import PartitionSpec as P

D = 16384
HD = 128
QH = 64
KVH = 4


rope_base = 500000.0
norm_eps = 1e-05


def rotate(values, positions):
    half_dim = values.shape[-1] // 2
    inverse = jnp.exp(
        jnp.arange(half_dim, dtype=jnp.float32) * (-2.0 * math.log(rope_base) / values.shape[-1])
    )
    angles = positions.astype(jnp.float32)[:, None] * inverse[None, :]
    cosine = jnp.cos(angles)
    sine_part = jnp.sin(angles)
    first_half = values[..., :half_dim]
    second_half = values[..., half_dim:]
    return jnp.concatenate(
        [
            first_half * cosine - second_half * sine_part,
            second_half * cosine + first_half * sine_part,
        ],
        axis=-1,
    )


def gathered_shards(activations, norm_gain, query_weight, kv_weight, out_weight, block_ids, clean_mask):
    row_count = lax.axis_size("row")
    col_index = lax.axis_index("col")
    seq_index = lax.axis_index("seq")
    slab_len = activations.shape[0]
    col_heads = query_weight.shape[1] // HD
    dev_heads = col_heads // row_count
    group_size = QH // KVH
    wide_input = activations.astype(jnp.float32)
    squares = lax.psum(jnp.sum(wide_input * wide_input, axis=1), ("row", "col"))
    scaling = lax.rsqrt(squares / D + norm_eps)
    normed = (wide_input * scaling[:, None] * norm_gain[None, :]).astype(jnp.bfloat16)
    panel_rows = lax.all_gather(normed, "col", axis=1, tiled=True)
    kv_count = max(col_heads // group_size, 1)
    kv_first = col_index * col_heads // group_size
    kv_tiles = lax.dynamic_slice_in_dim(kv_weight, kv_first * HD, kv_count * HD, 2)
    kv_term = jnp.einsum("td,dke->kte", panel_rows, kv_tiles, preferred_element_type=jnp.float32)
    columns = query_weight
    columns = columns.reshape(columns.shape[0], dev_heads * lax.axis_size("row"), HD)
    query_sum = lax.psum_scatter(
        jnp.einsum("td,dhe->hte", panel_rows, columns, preferred_element_type=jnp.float32),
        "row",
        scatter_dimension=0,
        tiled=True,
    )
    kv_sum = lax.psum(kv_term, "row")
    key_raw = kv_sum[0]
    value_rows = kv_sum[1].astype(jnp.bfloat16)
    positions = seq_index * slab_len + jnp.arange(slab_len, dtype=jnp.int32)
    key_rows = rotate(key_raw, positions).astype(jnp.bfloat16)
    queries = rotate(query_sum, positions).astype(jnp.bfloat16)
    my_blocks = lax.dynamic_slice_in_dim(block_ids, seq_index * slab_len, slab_len, 0)
    score_scale = 1.0 / math.sqrt(HD)
    key_piece = lax.all_gather(key_rows, "seq", axis=0, tiled=True)
    value_piece = lax.all_gather(value_rows, "seq", axis=0, tiled=True)
    visible = (block_ids[None, :] == my_blocks[:, None]) | (
        block_ids[None, :] < my_blocks[:, None]
    ) & (clean_mask[None, :] == 1)
    scores = (
        jnp.einsum("hte,ne->htn", queries, key_piece, preferred_element_type=jnp.float32)
        * score_scale
    )
    weights = jnp.where(visible[None, :, :], jnp.exp(scores), jnp.zeros_like(scores))
    numerator = jnp.einsum(
        "htn,ne->hte", weights.astype(jnp.bfloat16), value_piece, preferred_element_type=jnp.float32
    )
    denominator = jnp.sum(weights, axis=2)
    numerator, denominator = (numerator, denominator)
    attended = (numerator / denominator[:, :, None]).astype(jnp.bfloat16)
    out_cols = out_weight.shape[1]
    portion = lax.all_gather(attended, "row", axis=0, tiled=True)
    heads_here = portion.shape[0]
    out_rows = out_weight
    out_rows = out_rows.reshape(heads_here, HD, out_cols)
    partial_out = jnp.einsum("hte,hed->td", portion, out_rows, preferred_element_type=jnp.float32)
    projected = lax.psum_scatter(partial_out, "col", scatter_dimension=1, tiled=True)
    return projected.astype(jnp.bfloat16)


LINE = 4
OUTER_IN = ((0, 1), (3, 2))
OUTER_OUT = ((2, 3), (1, 0))
MIDDLE = ((1, 2), (2, 1))
DEST_ORDER = ((3, 2, 1, 0), (0, 3, 2, 1), (3, 0, 1, 2), (0, 1, 2, 3))
FEATURE_ORDER = ((0, 1, 2, 3), (1, 0, 2, 3), (2, 3, 1, 0), (3, 2, 1, 0))
CHUNK_SHARES = (12, 12, 8)
DEPTH = 512
BUFFERS = 4
COST_SCALE = 1.0
EXTRA = 16


def hop(values, pairs, axis="col"):
    return lax.ppermute(values, axis, list(pairs))


def chunk_bounds(slab):
    whole = sum(CHUNK_SHARES)
    marks = [slab * sum(CHUNK_SHARES[:i]) // whole // 16 * 16 for i in range(len(CHUNK_SHARES))] + [slab]
    return list(zip(marks[:-1], marks[1:]))


class Order:
    def __init__(self):
        self.token = []

    def call(self, body, outs, scratch, inputs, spaces, name, out_spaces=None, aliases=None, cost=1_000_000):
        count, given = len(inputs), len(outs)
        tokens = list(self.token)

        def kernel(*refs):
            refs = refs[:count] + refs[count + len(tokens) :]
            body(*refs[: count + given], *refs[count + given + 1 :])

        results = pl.pallas_call(
            kernel,
            out_shape=list(outs) + [jax.ShapeDtypeStruct((8, HD), jnp.float32)],
            in_specs=[pl.BlockSpec(memory_space=space) for space in spaces]
            + [pl.BlockSpec(memory_space=pl.ANY)] * len(tokens),
            out_specs=[pl.BlockSpec(memory_space=space) for space in (out_spaces or [pltpu.VMEM] * given)]
            + [pl.BlockSpec(memory_space=pl.ANY)],
            scratch_shapes=scratch,
            input_output_aliases=aliases or {},
            compiler_params=pltpu.CompilerParams(vmem_limit_bytes=36 << 20),
            cost_estimate=pl.CostEstimate(flops=0, bytes_accessed=int(cost * COST_SCALE), transcendentals=0),
            name=name,
        )(*inputs, *tokens)
        self.token = [results[-1]]
        return results[:-1]

    def arrive(self, *arrays):
        def body(*refs):
            pass

        outs = [jax.ShapeDtypeStruct(array.shape, array.dtype) for array in arrays]
        spaces = [pl.ANY] * len(arrays)
        return self.call(body, outs, [], arrays, spaces, "arrive", spaces, {i: i for i in range(len(arrays))}, 0)

    def add(self, groups, kinds):
        flat = [array for group in groups for array in group]

        def body(*refs):
            ins, outs = refs[: len(flat)], refs[len(flat) :]
            for group, out in zip(groups, outs):
                part, ins = ins[: len(group)], ins[len(group) :]
                out[...] = sum(ref[...].astype(jnp.float32) for ref in part).astype(out.dtype)

        outs = [jax.ShapeDtypeStruct(group[0].shape, kind) for group, kind in zip(groups, kinds)]
        return self.call(body, outs, [], flat, [pltpu.VMEM] * len(flat), "adding")


def last_sums(order, meta, first, third, fourth, through, inward_next):
    def body(meta_ref, first_ref, third_ref, through_ref, next_ref, outer, middle):
        @pl.when(meta_ref[4] == 1)
        def _():
            outer[...] = third_ref[...]

        @pl.when(meta_ref[4] == 0)
        def _():
            wide = first_ref[...].astype(jnp.float32) + through_ref[...].astype(jnp.float32)
            outer[...] = wide.astype(outer.dtype)

        wide = third_ref[...].astype(jnp.float32) + next_ref[...].astype(jnp.float32)
        middle[...] = wide.astype(middle.dtype)

    outer, middle = order.call(
        body,
        [jax.ShapeDtypeStruct(first.shape, first.dtype)] * 2,
        [],
        [meta, first, third, through, inward_next],
        [pltpu.SMEM] + [pltpu.VMEM] * 4,
        "last_sums",
    )
    return fourth, outer, middle


def gain_rows(order, activations, gain, rows):
    width = activations.shape[1]

    def body(source, gain_hbm, out, held, gain_ref, here):
        copies = [
            pltpu.make_async_copy(source.at[:rows, :], held, here.at[0]),
            pltpu.make_async_copy(gain_hbm, gain_ref, here.at[1]),
        ]
        for copy in copies:
            copy.start()
        for copy in copies:
            copy.wait()
        out[...] = (held[...].astype(jnp.float32) * gain_ref[...]).astype(out.dtype)

    return order.call(
        body,
        [jax.ShapeDtypeStruct((rows, width), jnp.bfloat16)],
        [
            pltpu.VMEM((rows, width), jnp.bfloat16),
            pltpu.VMEM(gain.shape, jnp.float32),
            pltpu.SemaphoreType.DMA((2,)),
        ],
        [activations, gain],
        [pl.ANY, pl.ANY],
        "gain_rows",
    )[0]


def key_value_terms(order, meta, activations, gain, weight, bounds):
    slab, width = activations.shape
    columns = weight.shape[1] * weight.shape[2]
    half = slab // 2
    steps = width // DEPTH

    def body(meta_ref, source, gain_ref, weight_ref, kept, given, *refs):
        outs, (gained, total, held, buffer, here, arrived) = refs[:-6], refs[-6:]
        brought = pltpu.make_async_copy(source, held, here)
        brought.start()

        def place(step):
            return pl.ds(meta_ref[10] * width + step * DEPTH, DEPTH)

        def multiply(step, block):
            @pl.when(step == 0)
            def _():
                brought.wait()
                wide = held[...].astype(jnp.float32)
                gained[...] = (wide * gain_ref[...]).astype(gained.dtype)
                total[...] = jnp.zeros_like(total)

            left = gained[:, pl.ds(pl.multiple_of(step * DEPTH, DEPTH), DEPTH)]
            total[...] += jnp.dot(left, block.reshape(DEPTH, columns), preferred_element_type=jnp.float32)

        streamed(weight_ref, place, steps, buffer, arrived, multiply)
        wide = held[...].astype(jnp.float32)
        squares = jnp.sum(wide * wide, axis=1, keepdims=True)
        diagonal = lax.broadcasted_iota(jnp.int32, (HD, HD), 0) == lax.broadcasted_iota(jnp.int32, (HD, HD), 1)
        for out, which in ((given, 1 - meta_ref[5]), (kept, meta_ref[5])):
            out[:half, :] = total[pl.ds(pl.multiple_of(which * half, half), half), :]
            out[half:, :] = jnp.zeros((EXTRA, columns), jnp.float32)
            for block in range(slab // HD):
                part = jnp.broadcast_to(squares[block * HD : (block + 1) * HD], (HD, HD))
                out[half : half + 1, block * HD : (block + 1) * HD] = jnp.sum(
                    jnp.where(diagonal, part, 0.0), axis=0, keepdims=True
                )
        for (low, high), out in zip(bounds, outs):
            out[...] = gained[low:high, :]

    kept, given, *gained = order.call(
        body,
        [jax.ShapeDtypeStruct((half + EXTRA, columns), jnp.float32)] * 2
        + [jax.ShapeDtypeStruct((high - low, width), jnp.bfloat16) for low, high in bounds],
        [
            pltpu.VMEM((slab, width), jnp.bfloat16),
            pltpu.VMEM((slab, columns), jnp.float32),
            pltpu.VMEM((slab, width), jnp.bfloat16),
            pltpu.VMEM((BUFFERS, DEPTH) + weight.shape[1:], jnp.bfloat16),
            pltpu.SemaphoreType.DMA(()),
            pltpu.SemaphoreType.DMA((BUFFERS,)),
        ],
        [meta, activations, gain, weight],
        [pltpu.SMEM, pl.ANY, pltpu.VMEM, pl.ANY],
        "key_value_terms",
        cost=15_000_000,
    )
    return kept, given, gained


def key_value_shares(order, meta, kept, arrived):
    rows, columns = kept.shape[0] - EXTRA, kept.shape[1]
    heads = columns // (2 * HD)

    def body(meta_ref, kept_ref, arrived_ref, *outs):
        squares = kept_ref[rows : rows + 1, :] + arrived_ref[rows : rows + 1, :]
        pieces, rest = [], squares
        for _ in range(3):
            piece = rest.astype(jnp.bfloat16)
            pieces.append(piece.astype(jnp.float32))
            rest = rest - pieces[-1]
        blocks = 2 * rows // HD
        lines = [
            jnp.concatenate([piece[:, i * HD : (i + 1) * HD] for piece in (pieces[0], pieces[1])], axis=1)
            for i in range(blocks)
        ] + [
            jnp.concatenate([pieces[2][:, i * HD : (i + 1) * HD]] * 2, axis=1) for i in range(blocks)
        ]
        lines = jnp.concatenate(lines + [jnp.zeros((EXTRA - 2 * blocks, 2 * HD), jnp.float32)], axis=0)
        for offset, out in enumerate(outs):
            head = lax.rem(meta_ref[10] + offset, heads)
            for part in range(2):
                spot = pl.ds(pl.multiple_of(part * heads * HD + head * HD, HD), HD)
                both = kept_ref[:rows, spot] + arrived_ref[:rows, spot]
                out[:rows, part * HD : (part + 1) * HD] = both.astype(out.dtype)
            out[rows:, :] = lines.astype(out.dtype)

    return order.call(
        body,
        [jax.ShapeDtypeStruct((rows + EXTRA, 2 * HD), jnp.float32)]
        + [jax.ShapeDtypeStruct((rows + EXTRA, 2 * HD), jnp.bfloat16)] * (heads - 1),
        [],
        [meta, kept, arrived],
        [pltpu.SMEM, pltpu.VMEM, pltpu.VMEM],
        "key_value_shares",
    )


def key_value_rows(order, meta, shares, cosine, sine):
    rows = shares[0].shape[0] - EXTRA
    blocks = 2 * rows // HD

    def body(meta_ref, *refs):
        share_refs, (cosine_ref, sine_ref, out, cosine_out, sine_out, scaling) = refs[: len(shares)], refs[len(shares) :]
        total = sum(ref[...].astype(jnp.float32) for ref in share_refs)
        diagonal = lax.broadcasted_iota(jnp.int32, (HD, HD), 0) == lax.broadcasted_iota(jnp.int32, (HD, HD), 1)
        for block in range(blocks):
            line = total[rows + block : rows + block + 1, :]
            last = total[rows + blocks + block : rows + blocks + block + 1, :HD]
            squares = line[:, :HD] + line[:, HD:] + last
            factor = lax.rsqrt(squares / D + norm_eps)
            column = jnp.sum(jnp.where(diagonal, factor, 0.0), axis=1, keepdims=True)
            scaling[block * HD : (block + 1) * HD, :] = jnp.broadcast_to(column, (HD, HD))
        cosine_out[...] = cosine_ref[...] * scaling[...]
        sine_out[...] = sine_ref[...] * scaling[...]
        spot = pl.ds(pl.multiple_of(meta_ref[5] * rows, rows), rows)
        raw = total[:rows, :HD]
        turned = pltpu.roll(raw, HD // 2, 1)
        out[:, :HD] = (raw * cosine_out[spot, :] + turned * sine_out[spot, :]).astype(out.dtype)
        out[:, HD:] = (total[:rows, HD:] * scaling[spot, :]).astype(out.dtype)

    inputs = [meta, *shares, cosine, sine]
    return order.call(
        body,
        [jax.ShapeDtypeStruct((rows, 2 * HD), jnp.bfloat16)] + [jax.ShapeDtypeStruct(cosine.shape, jnp.float32)] * 2,
        [pltpu.VMEM(cosine.shape, jnp.float32)],
        inputs,
        [pltpu.SMEM] + [pltpu.VMEM] * (len(inputs) - 1),
        "key_value_rows",
    )


def final_rows(order, so_far, slab, bounds, parts):
    rows, width = parts[0].shape

    def body(*refs):
        ins = refs[: len(parts)]
        out, held, here = refs[-3:]
        held[...] = sum(ref[...].astype(jnp.float32) for ref in ins).astype(held.dtype)
        copy = pltpu.make_async_copy(held, out.at[slice(*bounds), :], here)
        copy.start()
        copy.wait()

    inputs = list(parts) + ([] if so_far is None else [so_far])
    return order.call(
        body,
        [jax.ShapeDtypeStruct((slab, width), jnp.bfloat16)],
        [pltpu.VMEM((rows, width), jnp.bfloat16), pltpu.SemaphoreType.DMA(())],
        inputs,
        [pltpu.VMEM] * len(parts) + [pl.ANY] * (len(inputs) - len(parts)),
        "final_rows",
        [pl.ANY],
        {} if so_far is None else {len(parts): 0},
    )[0]


def streamed(weight_ref, place, steps, buffer, arrived, multiply):
    depth = buffer.shape[0]

    def copy(step):
        spot = lax.rem(step, depth)
        return pltpu.make_async_copy(weight_ref.at[place(step)], buffer.at[spot], arrived.at[spot])

    for step in range(min(depth, steps)):
        copy(jnp.int32(step)).start()

    def one(step, carry):
        copy(step).wait()
        multiply(step, buffer[lax.rem(step, depth)])

        @pl.when(step + depth < steps)
        def _():
            copy(step + depth).start()

        return carry

    lax.fori_loop(0, steps, one, 0)


def project(order, meta, slots, features, so_far, weight, split, kind=jnp.float32):
    rows, width = features[0].shape
    columns = weight.shape[1]
    steps = columns // DEPTH
    first, turns = slots[0][0], len(slots)

    def body(meta_ref, weight_ref, *refs):
        if so_far is not None:
            so_far_ref, refs = refs[0], refs[1:]
        feature_refs, refs = refs[: len(features)], refs[len(features) :]
        if split:
            outs, (total, held, buffer, here, arrived) = refs[:-5], refs[-5:]
        else:
            (total,), (held, buffer, here, arrived) = refs[:-4], refs[-4:]
        if so_far is not None:
            brought = pltpu.make_async_copy(so_far_ref, total, here.at[turns])
            brought.start()
        for turn, (_, choices) in enumerate(slots):
            def start(which):
                pltpu.make_async_copy(feature_refs[which], held.at[turn], here.at[turn]).start()

            if len(choices) == 1:
                start(choices[0])
            else:
                pl.when(meta_ref[4] == 0)(functools.partial(start, choices[0]))
                pl.when(meta_ref[4] == 1)(functools.partial(start, choices[1]))
        def place(step):
            rows_of = meta_ref[first + step // steps]
            return (
                pl.ds(pl.multiple_of(rows_of * width, width), width),
                pl.ds(pl.multiple_of(lax.rem(step, steps) * DEPTH, DEPTH), DEPTH),
            )

        def multiply(step, block):
            turn, inner = step // steps, lax.rem(step, steps)
            spot = pl.ds(pl.multiple_of(inner * DEPTH, DEPTH), DEPTH)

            if so_far is not None:
                pl.when(step == 0)(brought.wait)

            @pl.when(inner == 0)
            def _():
                pltpu.make_async_copy(feature_refs[0], held.at[turn], here.at[turn]).wait()

            part = jnp.dot(held[turn], block, preferred_element_type=jnp.float32)
            if so_far is not None:
                total[:, spot] += part
            else:
                @pl.when(turn == 0)
                def _():
                    total[:, spot] = part

                @pl.when(turn > 0)
                def _():
                    total[:, spot] += part

        streamed(weight_ref, place, turns * steps, buffer, arrived, multiply)
        if split:
            half = columns // 2
            mine = meta_ref[5]
            outs[0][...] = total[:, pl.ds(pl.multiple_of(mine * half, half), half)]
            outs[1][...] = total[:, pl.ds(pl.multiple_of((1 - mine) * half, half), half)].astype(outs[1].dtype)

    whole = jax.ShapeDtypeStruct((rows, columns), jnp.float32)
    halves = jax.ShapeDtypeStruct((rows, columns // 2), jnp.float32)
    inputs = [meta, weight] + ([] if so_far is None else [so_far]) + list(features)
    spaces = [pltpu.SMEM, pl.ANY] + ([] if so_far is None else [pl.ANY]) + [pl.ANY] * len(features)
    return order.call(
        body,
        [halves, jax.ShapeDtypeStruct(halves.shape, kind)] if split else [whole],
        ([pltpu.VMEM((rows, columns), jnp.float32)] if split else [])
        + [
            pltpu.VMEM((turns, rows, width), jnp.bfloat16),
            pltpu.VMEM((BUFFERS, width, DEPTH), jnp.bfloat16),
            pltpu.SemaphoreType.DMA((turns + 1,)),
            pltpu.SemaphoreType.DMA((BUFFERS,)),
        ],
        inputs,
        spaces,
        "project",
        cost=2 * turns * width * columns,
    )


def attend(order, mine, arrived, bounds, cosine, sine, pairs, own_ids, ids, cut):
    rows, width = mine.shape
    key_count = pairs.shape[0]
    tile = min(512, key_count)
    spot_rows = slice(*bounds)
    factor = math.log2(math.e) / math.sqrt(HD)

    def body(
        mine_ref, arrived_ref, cosine_ref, sine_ref, pair_ref, own_ids_ref, ids_ref, cut_ref, out_ref, bias, values
    ):
        values[:, :HD] = pair_ref[:, HD:]
        values[:, HD:] = jnp.ones((key_count, HD), values.dtype)
        own = own_ids_ref[spot_rows, :1]
        for first in range(0, key_count, tile):
            spot = slice(first, first + tile)
            seen = (ids_ref[:, spot] == own) | (cut_ref[:, spot] < own)
            bias[:, spot] = jnp.where(seen, 0.0, -jnp.inf)

        def one_head(head, carry):
            place = pl.ds(pl.multiple_of(head * HD, HD), HD)
            raw = mine_ref[:, place] + arrived_ref[:, place].astype(jnp.float32)
            turned = pltpu.roll(raw, HD // 2, 1)
            query = (raw * cosine_ref[spot_rows, :] + turned * sine_ref[spot_rows, :]).astype(jnp.bfloat16)
            summed = jnp.zeros((rows, values.shape[1]), jnp.float32)
            for first in range(0, key_count, tile):
                spot = slice(first, first + tile)
                scores = lax.dot_general(
                    query, pair_ref[spot, :HD], (((1,), (1,)), ((), ())), preferred_element_type=jnp.float32
                )
                weights = jnp.exp2(scores * factor + bias[:, spot])
                summed += jnp.dot(weights.astype(jnp.bfloat16), values[spot, :], preferred_element_type=jnp.float32)
            out_ref[:, place] = (summed[:, :HD] / summed[:, HD:]).astype(jnp.bfloat16)
            return carry

        lax.fori_loop(0, width // HD, one_head, 0, unroll=2)

    return order.call(
        body,
        [jax.ShapeDtypeStruct((rows, width), jnp.bfloat16)],
        [pltpu.VMEM((rows, key_count), jnp.float32), pltpu.VMEM((key_count, 2 * HD), jnp.bfloat16)],
        [mine, arrived, cosine, sine, pairs, own_ids, ids, cut],
        [pltpu.VMEM] * 8,
        "attend",
        cost=20_000_000,
    )[0]


def output_parts(order, meta, first_slot, mine, other, weight, kinds):
    rows, width = mine.shape
    depth = weight.shape[0]
    columns = weight.shape[1] // LINE
    steps = columns // DEPTH
    turns = len(kinds)

    def body(meta_ref, mine_ref, other_ref, weight_ref, *refs):
        outs, (*rounded, held, buffer, arrived, gone, here) = refs[:turns], refs[turns:]
        core = meta_ref[5]
        brought = [
            pltpu.make_async_copy(source, held.at[:, pl.ds(pl.multiple_of(which * width, width), width)], here.at[i])
            for i, (source, which) in enumerate(((mine_ref, core), (other_ref, 1 - core)))
        ]
        for copy in brought:
            copy.start()

        def leave(turn):
            return pltpu.make_async_copy(rounded[turn], outs[turn], gone.at[turn])

        def place(step):
            dest = meta_ref[6 + first_slot + step // steps]
            spot = dest * columns + lax.rem(step, steps) * DEPTH
            return (slice(None), pl.ds(pl.multiple_of(spot, DEPTH), DEPTH))

        def multiply(step, block):
            inner = lax.rem(step, steps)

            @pl.when(step == 0)
            def _():
                for copy in brought:
                    copy.wait()

            part = jnp.dot(held[...], block, preferred_element_type=jnp.float32)
            for turn in range(turns):
                @pl.when(step // steps == turn)
                def _():
                    spot = pl.ds(pl.multiple_of(inner * DEPTH, DEPTH), DEPTH)
                    rounded[turn][:, spot] = part.astype(rounded[turn].dtype)
                    pl.when(inner == steps - 1)(leave(turn).start)

        streamed(weight_ref, place, turns * steps, buffer, arrived, multiply)
        for turn in range(turns):
            leave(turn).wait()

    return order.call(
        body,
        [jax.ShapeDtypeStruct((rows, columns), kind) for kind in kinds],
        [
            *[pltpu.VMEM((rows, columns), kind) for kind in kinds],
            pltpu.VMEM((rows, depth), jnp.bfloat16),
            pltpu.VMEM((BUFFERS, depth, DEPTH), jnp.bfloat16),
            pltpu.SemaphoreType.DMA((BUFFERS,)),
            pltpu.SemaphoreType.DMA((turns,)),
            pltpu.SemaphoreType.DMA((2,)),
        ],
        [meta, mine, other, weight],
        [pltpu.SMEM, pl.ANY, pl.ANY, pl.ANY],
        "output_parts",
        [pl.ANY] * turns,
        cost=2 * turns * depth * columns,
    )


def line_shards(activations, norm_gain, query_weight, kv_weight, out_weight, block_ids, clean_mask):
    col, row, seq = (lax.axis_index(axis) for axis in ("col", "row", "seq"))
    slab, width = activations.shape
    bounds = chunk_bounds(slab)
    half = slab // 2
    swap = ((0, 1), (1, 0))
    at_end = (col == 0) | (col == LINE - 1)
    meta = jnp.concatenate(
        [
            jnp.asarray(FEATURE_ORDER, jnp.int32)[col],
            jnp.stack([at_end.astype(jnp.int32), row.astype(jnp.int32)]),
            jnp.asarray(DEST_ORDER, jnp.int32)[col],
            col[None],
        ]
    )

    def send_far(beside, across):
        return hop(beside, MIDDLE), hop(across, OUTER_OUT)

    ids = block_ids[None, :]
    cut = jnp.where(clean_mask == 1, block_ids, jnp.iinfo(jnp.int32).max)[None, :]
    my_ids = lax.dynamic_slice_in_dim(block_ids, seq * slab, slab, 0)
    my_ids = jnp.broadcast_to(my_ids[:, None], (slab, HD))

    inverse = jnp.exp(jnp.arange(HD // 2, dtype=jnp.float32) * (-2.0 * math.log(rope_base) / HD))
    positions = seq * slab + jnp.arange(slab, dtype=jnp.int32)
    angles = positions.astype(jnp.float32)[:, None] * inverse[None, :]
    rope_cosine = jnp.concatenate([jnp.cos(angles)] * 2, axis=1)
    rope_sine = jnp.concatenate([-jnp.sin(angles), jnp.sin(angles)], axis=1)

    order = Order()
    gain = norm_gain[None, :]
    first_rows = gain_rows(order, activations, gain, bounds[0][1])
    beside, across = hop(first_rows, OUTER_IN + OUTER_OUT), hop(first_rows, MIDDLE)

    around = [[(i, (i + offset) % LINE) for i in range(LINE)] for offset in range(1, LINE)]
    kept, given, gained = key_value_terms(order, meta, activations, gain, kv_weight, bounds[1:])
    gained = [first_rows] + gained
    given = hop(given, swap, "row")
    beside, across, my_ids, cut, rope_cosine, rope_sine = order.arrive(
        beside, across, my_ids, cut, rope_cosine, rope_sine
    )
    far = send_far(beside, across)
    own, *shares = key_value_shares(order, meta, kept, given)
    shares = [own] + [hop(share, pairs) for share, pairs in zip(shares, around)]
    pairs, cosine, sine = key_value_rows(order, meta, shares, rope_cosine, rope_sine)
    pairs = lax.all_gather(pairs, ("seq", "row"), axis=0, tiled=True)
    far_middle, far_end = order.arrive(*far)
    farthest = hop(far_middle, OUTER_OUT)

    out, waiting = None, None
    for i in range(len(bounds)):
        more = i + 1 < len(bounds)
        (so_far,) = project(
            order,
            meta,
            ((0, (0,)), (1, (1,)), (2, (2, 3))),
            (gained[i], beside, across, far_end),
            None,
            query_weight,
            False,
        )
        if more:
            farthest, gained[i + 1] = order.arrive(farthest, gained[i + 1])
            beside, across = hop(gained[i + 1], OUTER_IN + OUTER_OUT), hop(gained[i + 1], MIDDLE)
        mine, other = project(
            order, meta, ((3, (0, 1)),), (far_middle, farthest), so_far, query_weight, True, jnp.bfloat16 if i == 0 else jnp.float32
        )
        other = hop(other, swap, "row")
        if waiting is not None:
            fourth, outer, middle = last_sums(order, meta, *waiting)
            waiting = (fourth, hop(outer, OUTER_IN + OUTER_OUT), hop(middle, MIDDLE))
        attended = attend(order, mine, other, bounds[i], cosine, sine, pairs, my_ids, ids, cut)
        other_attended = hop(attended, swap, "row")
        if more:
            beside, across = order.arrive(beside, across)
            far_middle, far_end = send_far(beside, across)
        spread_out = lambda slot, *kinds: output_parts(
            order, meta, slot, attended, other_attended, out_weight, kinds
        )
        if more:
            first, second = spread_out(0, jnp.bfloat16, jnp.bfloat16)
            inward, inward_next = hop(first, OUTER_IN), hop(second, OUTER_IN)
            third, fourth = spread_out(2, jnp.bfloat16, jnp.float32)
        else:
            (first,) = spread_out(0, jnp.bfloat16)
            inward = hop(first, OUTER_IN)
            second, third, fourth = spread_out(1, jnp.bfloat16, jnp.bfloat16, jnp.float32)
            inward_next = hop(second, OUTER_IN)
        if waiting is not None:
            out = final_rows(order, out, slab, bounds[i - 1], waiting)
        if more:
            far_middle, far_end = order.arrive(far_middle, far_end)
            farthest = hop(far_middle, OUTER_OUT)
        (middle,) = order.add([(second, inward)], [jnp.bfloat16])
        waiting = (first, third, fourth, hop(middle, MIDDLE), inward_next)
    inward_last = hop(waiting[1], OUTER_IN)
    fourth, outer, middle = last_sums(order, meta, *waiting)
    outer, middle = hop(outer, OUTER_OUT), hop(middle, MIDDLE)
    return final_rows(order, out, slab, bounds[-1], (fourth, inward_last, outer, middle))


def solution(mesh):
    placed = (
        P("seq", ("row", "col")),
        P(("row", "col")),
        P("row", "col"),
        P("row", None, None),
        P("col", "row"),
        P(),
        P(),
    )
    on_line = mesh.shape["col"] == LINE == KVH and mesh.shape["row"] == 2
    return jax.shard_map(
        line_shards if on_line else gathered_shards,
        mesh=mesh,
        in_specs=placed,
        out_specs=P("seq", ("row", "col")),
        check_vma=False,
    )
```
